256 devices in a mesh: ctx: 128 (over x, y, z_lo, core), head: 2 (over z_hi).
Axes of the slice: x: 4, y: 4, z: 8 (z_hi: 2, z_lo: 4; z = z_hi * 4 + z_lo), core: 2. Of those that a mesh axis runs over, the one named last changes fastest.
Arguments:
- latent: bfloat16 [16384, 512], P('ctx'), may hold values from -6 to 6
- rope_key: bfloat16 [16384, 64], P('ctx'), may hold values from -6 to 6
- queries: bfloat16 [16384, 64, 512], P('ctx', 'head'), may hold values from -89 to 89
- query_rope: bfloat16 [16384, 4096], P('ctx', 'head'), may hold values from -6 to 6
- grad_out: bfloat16 [16384, 64, 512], P('ctx', 'head'), may hold values from -6 to 6
- sel_blocks: int32 [256, 5], P('ctx'), may hold values from 0 to 255, as said below
Outputs:
- attention_out: bfloat16 [16384, 64, 512], P('ctx', 'head')
- d_latent: float32 [16384, 512], P('ctx')
- d_rope_key: float32 [16384, 64], P('ctx')
The draws below stay inside these ranges and needn't reach their ends.
Inputs may be any that keep to these rules, and one draw needn't show every extreme that they name: `sel_blocks`: row b lists the key blocks of query block b: slot 0 holds b, slots 1 to min(b, 4) hold distinct blocks below b, any of them, and any later slots hold b and are not used.
All inputs are finite; a program needn't handle non-finite values.
Results may differ from the reference program's by a relative error of at most 0.007.
Values may be sent and summed in bfloat16 or wider, within the bound.
No kernel may reach another device: no remote copies, remote signals or barrier semaphores. Data moves between devices by JAX's collectives and lax.ppermute only.
A program may use at most 192 MiB of HBM per device.

```python
import jax
import jax.numpy as jnp
from jax import lax

HEADS = 64
LAT = 512
ROPE = 64
BLK = 64
SEL = 5
TOKENS = 16384
SEGMENT_TOTAL = 256


def draw_latent(key, part):
    key = jax.random.fold_in(key, 3)
    values = jnp.clip(jax.random.normal(key, (TOKENS, LAT), jnp.float32), -6.0, 6.0)
    return values.astype(jnp.bfloat16)


def draw_queries(key, part):
    key = jax.random.fold_in(key, 5)
    values = jnp.clip(jax.random.normal(key, (TOKENS, HEADS, LAT), jnp.float32), -6.0, 6.0)
    return values.astype(jnp.bfloat16)


def draw_sel_blocks(key, part):
    key = jax.random.fold_in(key, 11)
    primary_sampler_seed, extra_sampler_seed = jax.random.split(key)
    row_ids = jnp.arange(SEGMENT_TOTAL, dtype=jnp.int32)[:, None]
    segment_positions_list = jnp.arange(SEGMENT_TOTAL, dtype=jnp.int32)[None, :]
    primary_weights = jax.random.randint(primary_sampler_seed, (SEGMENT_TOTAL, SEGMENT_TOTAL), 0, 4096, jnp.int32)
    preferred_segments = ((segment_positions_list == 0) | (row_ids - segment_positions_list <= 2)).astype(jnp.int32)
    extra_weights = jax.random.randint(extra_sampler_seed, (SEGMENT_TOTAL, SEGMENT_TOTAL), 0, 2, jnp.int32) * 4096 * preferred_segments
    segment_order = (primary_weights + extra_weights) * SEGMENT_TOTAL + segment_positions_list
    segment_order = jnp.where(segment_positions_list < row_ids, segment_order, -1 - segment_positions_list)
    chosen = lax.top_k(segment_order, SEL - 1)[1].astype(jnp.int32)
    slot_ids = jnp.arange(1, SEL, dtype=jnp.int32)[None, :]
    chosen = jnp.where(slot_ids <= row_ids, chosen, row_ids)
    own_block = jnp.broadcast_to(row_ids, (SEGMENT_TOTAL, 1))
    return jnp.concatenate([own_block, chosen], axis=1).astype(jnp.int32)


def block_levels(stream_key, dims, shards, least, high):
    loudness, own = 1.0, jax.random.fold_in(stream_key, 6)
    for position, blocks in shards:
        draws = jnp.exp(jax.random.uniform(jax.random.fold_in(own, position), (blocks,), jnp.float32, least / len(shards), high / len(shards)))
        loudness = loudness * jnp.repeat(draws, dims[position] // blocks).reshape([-1 if axis == position else 1 for axis in range(len(dims))])
    return loudness


def noise(stream_key, extent, width, most, cuts=(), kind=jnp.bfloat16):
    loudness = block_levels(stream_key, extent, cuts, -0.22, 0.18) if cuts else 1.0
    values = jax.random.normal(stream_key, extent, jnp.float32) * width * loudness
    return jnp.minimum(jnp.maximum(values, -most), most).astype(kind)


def setup_inputs(seed: int = 0) -> dict:
    splits = jax.random.split(jax.random.key(seed), 7)
    latent = draw_latent(jax.random.fold_in(splits[6], 71), 0)
    rope_key = noise(splits[1], (TOKENS, ROPE), 1.0, 6.0, ((0, 128),))
    queries = draw_queries(jax.random.fold_in(splits[6], 71), 0)
    query_rope = noise(splits[3], (TOKENS, HEADS * ROPE), 1.0, 6.0, ((0, 128), (1, 2)))
    grad_out = noise(splits[4], (TOKENS, HEADS, LAT), 1.0, 6.0, ((0, 128), (1, 2)))
    sel_blocks = draw_sel_blocks(jax.random.fold_in(splits[6], 71), 0)
    return dict(latent=latent, rope_key=rope_key, queries=queries, query_rope=query_rope, grad_out=grad_out, sel_blocks=sel_blocks)


softmax_scale = 192.0 ** -0.5
rope_base = 10000.0


def rotate_pairs(values, positions, direction):
    half_width = values.shape[-1] // 2
    freq_steps = jnp.arange(half_width, dtype=jnp.float32)
    inverse_freq = rope_base ** (-2.0 * freq_steps / values.shape[-1])
    angles = positions.astype(jnp.float32)[:, None] * inverse_freq[None, :]
    cosine = jnp.cos(angles)
    sine_part = jnp.sin(angles) * direction
    lower_half = values[:, :half_width]
    upper_half = values[:, half_width:]
    return jnp.concatenate([lower_half * cosine - upper_half * sine_part, upper_half * cosine + lower_half * sine_part], axis=1)


def reference(latent, rope_key, queries, query_rope, grad_out, sel_blocks):
    positions = jnp.arange(TOKENS, dtype=jnp.int32)
    rotated = rotate_pairs(rope_key.astype(jnp.float32), positions, 1.0).astype(jnp.bfloat16)
    offsets = jnp.arange(BLK, dtype=jnp.int32)
    slot_index = jnp.arange(SEL * BLK, dtype=jnp.int32) // BLK

    def one_block(carry, block_index):
        selected = sel_blocks[block_index]
        key_rows = (selected[:, None] * BLK + offsets[None, :]).reshape(-1).astype(jnp.int32)
        latent_key_rows = latent[key_rows].astype(jnp.float32)
        keys_rotated = rotated[key_rows].astype(jnp.float32)
        first_row = (block_index * BLK).astype(jnp.int32)
        latent_query_rows = lax.dynamic_slice_in_dim(queries, first_row, BLK, 0).astype(jnp.float32)
        query_rotary = lax.dynamic_slice_in_dim(query_rope, first_row, BLK, 0).reshape(BLK, HEADS, ROPE).astype(jnp.float32)
        upstream_gradient = lax.dynamic_slice_in_dim(grad_out, first_row, BLK, 0).astype(jnp.float32)
        scores = (jnp.einsum("thd,kd->thk", latent_query_rows, latent_key_rows) + jnp.einsum("thr,kr->thk", query_rotary, keys_rotated)) * softmax_scale
        slot_valid = slot_index < jnp.minimum(block_index + 1, SEL)
        query_pos = first_row + offsets
        allowed = slot_valid[None, :] & (key_rows[None, :] <= query_pos[:, None])
        scores = jnp.where(allowed[:, None, :], scores, -jnp.inf)
        row_max = jnp.max(scores, axis=-1, keepdims=True)
        expon = jnp.exp(scores - row_max)
        probs = expon / jnp.sum(expon, axis=-1, keepdims=True)
        probability_lowered = lax.optimization_barrier(probs.astype(jnp.bfloat16)).astype(jnp.float32)
        block_out = jnp.einsum("thk,kd->thd", probability_lowered, latent_key_rows).astype(jnp.bfloat16)
        dprobs = jnp.einsum("thd,kd->thk", upstream_gradient, latent_key_rows)
        row_delta = jnp.sum(probs * dprobs, axis=-1, keepdims=True)
        scores_gradient = lax.optimization_barrier((probs * (dprobs - row_delta)).astype(jnp.bfloat16)).astype(jnp.float32)
        grad_latent = softmax_scale * jnp.einsum("thk,thd->kd", scores_gradient, latent_query_rows) + jnp.einsum("thk,thd->kd", probability_lowered, upstream_gradient)
        grad_rotary = softmax_scale * jnp.einsum("thk,thr->kr", scores_gradient, query_rotary)
        carry = carry.at[key_rows].add(jnp.concatenate([grad_latent, grad_rotary], axis=1))
        return carry, block_out

    initial = jnp.zeros((TOKENS, LAT + ROPE), jnp.float32)
    key_grad, outputs = lax.scan(one_block, initial, jnp.arange(SEGMENT_TOTAL, dtype=jnp.int32))
    attention_out = outputs.reshape(TOKENS, HEADS, LAT)
    d_latent = key_grad[:, :LAT]
    d_rope_key = rotate_pairs(key_grad[:, LAT:], positions, -1.0)
    return attention_out, d_latent, d_rope_key
```

```python
import functools

import jax
import jax.numpy as jnp
from jax import lax
from jax.experimental import pallas as pl
from jax.experimental.pallas import tpu as pltpu
from jax.sharding import Mesh, PartitionSpec as P

BLK = 64
SEL = 5
LAT = 512
ROPE = 64
HEADS = 32
UNIT = 16
HALF = 144
TILE = 512

softmax_scale = 192.0 ** (-0.5)
rope_base = 10000.0

bf16 = jnp.bfloat16
f32 = jnp.float32
VMEM = pl.BlockSpec(memory_space=pltpu.VMEM)
SMEM = pl.BlockSpec(memory_space=pltpu.SMEM)
PARAMS = pltpu.CompilerParams(vmem_limit_bytes=48 * 1024 * 1024)


def call(kernel, ins, outs, scratch=(), scalars=0, name=None):
    specs = [SMEM] * scalars + [VMEM] * (len(ins) - scalars)
    return pl.pallas_call(
        kernel,
        out_shape=[jax.ShapeDtypeStruct(s, d) for s, d in outs],
        in_specs=specs,
        out_specs=[VMEM] * len(outs),
        scratch_shapes=list(scratch),
        compiler_params=PARAMS,
        name=name,
    )(*ins)


MESH = ("x", "y", "z", "c", "h")


def partner(place, phase, k):
    x, y, z, c, h = place
    axis = "z" if phase == "u" else "xy"[c if phase == "v" else 1 - c]
    if axis == "x":
        x ^= k
    elif axis == "y":
        y ^= k
    else:
        ring = h * 4 + z
        if k == 3:
            ring = (ring + (1 if ring % 2 else 7)) % 8
        else:
            ring ^= k
        h, z = ring // 4, ring % 4
    return x, y, z, c, h


def number(place):
    x, y, z, c, h = place
    return (((x * 4 + y) * 4 + z) * 2 + c) * 2 + h


def exchange(a, phase, k):
    places = [(i // 64, i // 16 % 4, i // 4 % 4, i // 2 % 2, i % 2) for i in range(256)]
    return lax.ppermute(a, MESH, [(number(p), number(partner(p, phase, k))) for p in places])


def swap(a, axis):
    return lax.ppermute(a, axis, [(0, 1), (1, 0)])


def prep_kernel(meta, lat, rope, cosine, sine, sel, mine, other, rot_out, units):
    c = meta[0]
    x = rope[...].astype(f32)
    lo, hi = x[:, :32], x[:, 32:]
    rot = jnp.concatenate(
        [lo * cosine[...] - hi * sine[...], hi * cosine[...] + lo * sine[...]], axis=1
    ).astype(bf16)
    rot_out[...] = rot
    for i in range(2):
        packed = jnp.concatenate([rot[i * 64 : i * 64 + 32], rot[i * 64 + 32 : i * 64 + 64]], axis=1)
        for n in range(18):
            if n < 16:
                l, r = n // 4, n % 4
                v = lat[i * 64 + r * UNIT : i * 64 + (r + 1) * UNIT, l * 128 : (l + 1) * 128]
            else:
                v = packed[(n - 16) * UNIT : (n - 15) * UNIT]
            row = i * HALF + (n % 9) * UNIT
            units[n // 9, row : row + UNIT, :] = v
    for half in range(2):
        units[half, 288:304, :] = sel[...]
    mine[...] = units[c]
    other[...] = units[1 - c]


def chip_kernel(mine, recv, x, sel):
    x[0:288] = mine[0:288]
    x[288:576] = recv[0:288]
    row = lax.broadcasted_iota(jnp.int32, (UNIT, 128), 0)
    sel[...] = jnp.where(
        row == 0, mine[288:304].astype(f32), recv[288:304].astype(f32)
    ).astype(bf16)


def line_kernel(*refs):
    for k in range(4):
        refs[4][k * 576 : (k + 1) * 576] = refs[k][...]


def pack_kernel(where_, *refs):
    ins, outs, held = refs[:4], refs[4:8], refs[8]
    for k in range(4):
        held[k * 16 : (k + 1) * 16] = ins[k][...].reshape(16, HALF, 128)
    for k in range(4):
        for s in range(16):
            outs[k][s * HALF : (s + 1) * HALF] = held[where_[k * 16 + s]]


def merge_kernel(where_, *refs):
    ins, mine, other, held = refs[:4], refs[4], refs[5], refs[6]
    for k in range(4):
        held[k * 16 : (k + 1) * 16] = ins[k][...].reshape(16, HALF, 128)
    for s in range(16):
        out = mine if s < 8 else other
        row = (s % 8) * HALF
        out[row : row + HALF] = held[where_[s] * 16 + s]


def attention_kernel(
    meta, lat, rot, mine, other, q_ref, qr_ref, do_ref,
    out_ref, dkl_ref, dkr_ref, gm_ref, go_ref,
    units, keys, keys_r, acc, acc_r,
):
    i, t = pl.program_id(0), pl.program_id(1)
    c = meta[0]
    block = meta[1] + i

    @pl.when(t == 0)
    def _():
        rows = pl.ds(pl.multiple_of(i * BLK, BLK), BLK)
        keys[0:BLK] = lat[rows, :]
        keys_r[0:BLK] = rot[rows, :]
        part = pl.ds(pl.multiple_of(i * 576, 576), 576)
        units[c] = mine[part, :]
        units[1 - c] = other[part, :]
        for s in range(4):
            base = (s + 1) * BLK
            for n in range(16):
                row = s * HALF + (n % 9) * UNIT
                l, r = n // 4, n % 4
                keys[base + r * UNIT : base + (r + 1) * UNIT, l * 128 : (l + 1) * 128] = units[
                    n // 9, row : row + UNIT, :
                ]
            packed = units[1, s * HALF + 112 : s * HALF + 144, :]
            keys_r[base : base + 32] = packed[:, :64]
            keys_r[base + 32 : base + 64] = packed[:, 64:]
        acc[...] = jnp.zeros_like(acc)
        acc_r[...] = jnp.zeros_like(acc_r)

    q, qr, do = q_ref[...], qr_ref[...], do_ref[...]
    nt = (((1,), (1,)), ((), ()))
    raw = lax.dot_general(keys[...], q, nt, preferred_element_type=f32)
    raw = raw + lax.dot_general(keys_r[...], qr, nt, preferred_element_type=f32)
    key_row = lax.broadcasted_iota(jnp.int32, raw.shape, 0)
    query = lax.broadcasted_iota(jnp.int32, raw.shape, 1) // HEADS + t * (TILE // HEADS)
    limit = jnp.minimum(block + 1, SEL) * BLK
    allowed = (key_row < limit) & ((key_row >= BLK) | (key_row <= query))
    raw = jnp.where(allowed, raw, -jnp.inf)
    top = jnp.max(raw, axis=0, keepdims=True)
    expon = jnp.exp((raw - top) * softmax_scale)
    probs = expon * (1.0 / jnp.sum(expon, axis=0, keepdims=True))
    probs_low = probs.astype(bf16)
    dprobs = lax.dot_general(keys[...], do, nt, preferred_element_type=f32)
    row_delta = jnp.sum(probs * dprobs, axis=0, keepdims=True)
    dscores = (probs * (dprobs - row_delta) * softmax_scale).astype(bf16)
    out_ref[...] = lax.dot_general(
        probs_low, keys[...], (((0,), (0,)), ((), ())), preferred_element_type=f32
    ).astype(bf16)
    acc[...] += jnp.dot(dscores, q, preferred_element_type=f32) + jnp.dot(
        probs_low, do, preferred_element_type=f32
    )
    acc_r[...] += jnp.dot(dscores, qr, preferred_element_type=f32)

    @pl.when(t == pl.num_programs(1) - 1)
    def _():
        rows = pl.ds(pl.multiple_of(i * BLK, BLK), BLK)
        dkl_ref[rows, :] = acc[0:BLK]
        dkr_ref[rows, :] = acc_r[0:BLK]
        for s in range(4):
            base = (s + 1) * BLK
            packed = jnp.concatenate(
                [acc_r[base : base + 32, :], acc_r[base + 32 : base + 64, :]], axis=1
            )
            for n in range(18):
                m = n % 9
                if n < 16:
                    l, r = n // 4, n % 4
                    v = acc[base + r * UNIT : base + (r + 1) * UNIT, l * 128 : (l + 1) * 128]
                else:
                    v = packed[(n - 16) * UNIT : (n - 15) * UNIT]
                row = s * HALF + m * UNIT
                units[n // 9, row : row + UNIT, :] = v.astype(bf16)
        part = pl.ds(pl.multiple_of(i * 576, 576), 576)
        gm_ref[part, :] = units[c]
        go_ref[part, :] = units[1 - c]


def attention(meta, lat, rot, mine, other, q, qr, do):
    tiles = BLK * HEADS // TILE
    whole = lambda shape: pl.BlockSpec(shape, lambda i, t: (0, 0))
    rows = lambda width: pl.BlockSpec((TILE, width), lambda i, t: (i * tiles + t, 0))
    return pl.pallas_call(
        attention_kernel,
        grid=(2, tiles),
        out_shape=[
            jax.ShapeDtypeStruct(q.shape, bf16),
            jax.ShapeDtypeStruct((128, LAT), f32),
            jax.ShapeDtypeStruct((128, ROPE), f32),
            jax.ShapeDtypeStruct((8 * HALF, 128), bf16),
            jax.ShapeDtypeStruct((8 * HALF, 128), bf16),
        ],
        in_specs=[
            SMEM,
            whole((128, LAT)),
            whole((128, ROPE)),
            whole((8 * HALF, 128)),
            whole((8 * HALF, 128)),
            rows(LAT),
            rows(ROPE),
            rows(LAT),
        ],
        out_specs=[
            rows(LAT),
            whole((128, LAT)),
            whole((128, ROPE)),
            whole((8 * HALF, 128)),
            whole((8 * HALF, 128)),
        ],
        scratch_shapes=[
            pltpu.VMEM((2, 576, 128), bf16),
            pltpu.VMEM((SEL * BLK, LAT), bf16),
            pltpu.VMEM((SEL * BLK, ROPE), bf16),
            pltpu.VMEM((SEL * BLK, LAT), f32),
            pltpu.VMEM((SEL * BLK, ROPE), f32),
        ],
        compiler_params=PARAMS,
        name="attention",
    )(meta, lat, rot, mine, other, q, qr, do)


def slots_kernel(mine, recv, g):
    g[0:1152] = mine[...]
    g[1152:2304] = recv[...]


def plane_kernel(where_, *refs):
    ins, outs, acc = refs[:4], refs[4:8], refs[8]
    acc[...] = jnp.zeros_like(acc)
    for k in range(4):
        for s in range(16):
            f = where_[k * 16 + s]
            acc[f] = acc[f] + ins[k][s * HALF : (s + 1) * HALF].astype(f32)
    for k in range(4):
        for j in range(16):
            outs[k][j * HALF : (j + 1) * HALF] = acc[k * 16 + j].astype(outs[k].dtype)


def sum_rows(ins, at):
    total = ins[0][at : at + HALF]
    for k in range(1, 4):
        total = total + ins[k][at : at + HALF].astype(f32)
    return total


def column_kernel(*refs):
    ins, outs = refs[:4], refs[4:8]
    for j in range(16):
        out, row = outs[j // 4], (j % 4) * HALF
        out[row : row + HALF] = sum_rows(ins, j * HALF).astype(out.dtype)


def owner_kernel(*refs):
    ins, outs = refs[:4], refs[4:6]
    for j in range(4):
        row = (j % 2) * HALF
        outs[j // 2][row : row + HALF] = sum_rows(ins, j * HALF)


def half_sum_kernel(meta, mine, recv, dkl, dkr, out, units):
    c = meta[0]
    units[c] = mine[...]
    units[1 - c] = recv[...]
    for i in range(2):
        lo, hi = slice(i * 64, i * 64 + 32), slice(i * 64 + 32, i * 64 + 64)
        packed = jnp.concatenate([dkr[lo, :], dkr[hi, :]], axis=1)
        for n in range(18):
            if n < 16:
                l, r = n // 4, n % 4
                own = dkl[i * 64 + r * UNIT : i * 64 + (r + 1) * UNIT, l * 128 : (l + 1) * 128]
            else:
                own = packed[(n - 16) * UNIT : (n - 15) * UNIT]
            row = i * HALF + (n % 9) * UNIT
            to = (i * 18 + n) * UNIT
            out[to : to + UNIT] = (units[n // 9, row : row + UNIT, :] + own).astype(bf16)


def final_kernel(mine, recv, cosine, sine, lat_out, rope_out):
    for i in range(2):
        for n in range(16):
            l, r = n // 4, n % 4
            at = (i * 18 + n) * UNIT
            lat_out[i * 64 + r * UNIT : i * 64 + (r + 1) * UNIT, l * 128 : (l + 1) * 128] = mine[
                at : at + UNIT
            ].astype(f32) + recv[at : at + UNIT].astype(f32)
        at = (i * 18 + 16) * UNIT
        packed = mine[at : at + 32].astype(f32) + recv[at : at + 32].astype(f32)
        for part in range(2):
            rows = slice(i * 64 + part * 32, i * 64 + part * 32 + 32)
            g = packed[:, part * 64 : part * 64 + 64]
            lo, hi = g[:, :32], g[:, 32:]
            cs, sn = cosine[rows, :], sine[rows, :]
            rope_out[rows, :] = jnp.concatenate([lo * cs + hi * sn, hi * cs - lo * sn], axis=1)


def shards(latent, rope_key, queries, query_rope, grad_out, sel_blocks):
    x, y, z, c = [lax.axis_index(a) for a in "xyzc"]
    ctx = ((x * 4 + y) * 4 + z) * 2 + c
    meta = jnp.stack([c, ctx * 2]).astype(jnp.int32)

    positions = ctx * 128 + jnp.arange(128, dtype=jnp.int32)
    freq_steps = jnp.arange(ROPE // 2, dtype=f32)
    inverse_freq = rope_base ** (-2.0 * freq_steps / ROPE)
    angles = positions.astype(f32)[:, None] * inverse_freq[None, :]
    cosine, sine = jnp.cos(angles), jnp.sin(angles)

    sel_row = sel_blocks[:, 1:].reshape(1, 8).astype(bf16)
    sel_unit = jnp.broadcast_to(jnp.pad(sel_row, ((0, 0), (0, 120))), (UNIT, 128))
    mine, other, rot = call(
        prep_kernel,
        (meta, latent, rope_key, cosine, sine, sel_unit),
        [((304, 128), bf16), ((304, 128), bf16), ((128, ROPE), bf16)],
        [pltpu.VMEM((2, 304, 128), bf16)],
        scalars=1,
        name="prep",
    )
    chip, sel = call(
        chip_kernel, (mine, swap(other, "c")), [((576, 128), bf16), ((UNIT, 128), bf16)], name="chip"
    )

    def all_of(a, phase):
        return [a] + [exchange(a, phase, k) for k in (1, 2, 3)]

    lines = all_of(chip, "u")
    (line,) = call(line_kernel, lines, [((2304, 128), bf16)], name="line")
    planes = all_of(line, "v")

    asked = jnp.stack([t[:2, :8] for t in all_of(sel, "w")]).astype(jnp.int32).reshape(4, 16)
    sx, sy, sz = asked >> 6, (asked >> 4) & 3, (asked >> 2) & 3
    local = jnp.where(((asked >> 1) & 1) == c, 0, 2) + (asked & 1)
    on_v = jnp.where(c == 0, x ^ sx, y ^ sy)
    on_w = jnp.where(c == 0, y ^ sy, x ^ sx)
    pos = on_v * 16 + (z ^ sz) * 4 + local
    pack_at = pos.reshape(-1)
    add_at = jnp.where(on_w == 0, pos, 64).reshape(-1)
    merge_at = on_w[0]

    packed = call(
        pack_kernel,
        [pack_at] + planes,
        [((2304, 128), bf16)] * 4,
        [pltpu.VMEM((64, HALF, 128), bf16)],
        scalars=1,
        name="pack",
    )
    got = [packed[0]] + [exchange(packed[k], "w", k) for k in (1, 2, 3)]
    key_mine, key_other = call(
        merge_kernel,
        [merge_at] + got,
        [((8 * HALF, 128), bf16)] * 2,
        [pltpu.VMEM((64, HALF, 128), bf16)],
        scalars=1,
        name="merge",
    )
    key_recv = swap(key_other, "c")

    q = queries.reshape(128 * HEADS, LAT)
    do = grad_out.reshape(128 * HEADS, LAT)
    qr = query_rope.reshape(128 * HEADS, ROPE)
    out, dkl, dkr, g_mine, g_other = attention(meta, latent, rot, key_mine, key_recv, q, qr, do)

    (slots,) = call(slots_kernel, (g_mine, swap(g_other, "c")), [((2304, 128), bf16)], name="slots")
    sums = call(
        plane_kernel,
        [add_at] + all_of(slots, "w"),
        [((2304, 128), bf16 if k else f32) for k in range(4)],
        [pltpu.VMEM((65, HALF, 128), f32)],
        scalars=1,
        name="plane",
    )
    got = [sums[0]] + [exchange(sums[k], "v", k) for k in (1, 2, 3)]
    sums = call(column_kernel, got, [((576, 128), bf16 if k else f32) for k in range(4)], name="column")
    got = [sums[0]] + [exchange(sums[k], "u", k) for k in (1, 2, 3)]
    f_mine, f_other = call(owner_kernel, got, [((288, 128), f32)] * 2, name="owner")
    (total,) = call(
        half_sum_kernel,
        (meta, f_mine, swap(f_other, "c"), dkl, dkr),
        [((576, 128), bf16)],
        [pltpu.VMEM((2, 288, 128), f32)],
        scalars=1,
        name="half_sum",
    )
    d_latent, d_rope_key = call(
        final_kernel,
        (total, swap(total, "h"), cosine, sine),
        [((128, LAT), f32), ((128, ROPE), f32)],
        name="final",
    )
    return out.reshape(128, HEADS, LAT), d_latent, d_rope_key


def solution(mesh):
    lines = Mesh(mesh.devices.reshape(4, 4, 4, 2, 2), MESH)
    ctx = ("x", "y", "z", "c")
    return jax.shard_map(
        shards,
        mesh=lines,
        in_specs=(
            P(ctx, None),
            P(ctx, None),
            P(ctx, "h", None),
            P(ctx, "h"),
            P(ctx, "h", None),
            P(ctx, None),
        ),
        out_specs=(P(ctx, "h", None), P(ctx, None), P(ctx, None)),
        check_vma=False,
    )
```

```python
import functools

import jax
import jax.numpy as jnp
from jax import lax
from jax.experimental import pallas as pl
from jax.experimental.pallas import tpu as pltpu
from jax.sharding import Mesh, PartitionSpec as P

BLK = 64
SEL = 5
LAT = 512
ROPE = 64
HEADS = 32
UNIT = 16
HALF = 144
ORDER = (0, 3, 2, 1)
DISTANCES = (1, 2, 3)
TILE = 512

softmax_scale = 192.0 ** (-0.5)
rope_base = 10000.0

bf16 = jnp.bfloat16
f32 = jnp.float32
VMEM = pl.BlockSpec(memory_space=pltpu.VMEM)
SMEM = pl.BlockSpec(memory_space=pltpu.SMEM)
PARAMS = pltpu.CompilerParams(vmem_limit_bytes=48 * 1024 * 1024)


def call(kernel, ins, outs, scratch=(), scalars=0, name=None):
    specs = [SMEM] * scalars + [VMEM] * (len(ins) - scalars)
    return pl.pallas_call(
        kernel,
        out_shape=[jax.ShapeDtypeStruct(s, d) for s, d in outs],
        in_specs=specs,
        out_specs=[VMEM] * len(outs),
        scratch_shapes=list(scratch),
        compiler_params=PARAMS,
        name=name,
    )(*ins)


MESH = ("x", "y", "z", "c", "h")


def partner(place, phase, k):
    x, y, z, c, h = place
    axis = "z" if phase == "u" else "xy"[c if phase == "v" else 1 - c]
    if axis == "x":
        x ^= k
    elif axis == "y":
        y ^= k
    else:
        ring = h * 4 + z
        if k == 3:
            ring = (ring + (1 if ring % 2 else 7)) % 8
        else:
            ring ^= k
        h, z = ring // 4, ring % 4
    return x, y, z, c, h


def number(place):
    x, y, z, c, h = place
    return (((x * 4 + y) * 4 + z) * 2 + c) * 2 + h


def exchange(a, phase, k):
    places = [(i // 64, i // 16 % 4, i // 4 % 4, i // 2 % 2, i % 2) for i in range(256)]
    return lax.ppermute(a, MESH, [(number(p), number(partner(p, phase, k))) for p in places])


def swap(a, axis):
    return lax.ppermute(a, axis, [(0, 1), (1, 0)])


def prep_kernel(meta, lat, rope, cosine, sine, sel, mine, other, rot_out, units):
    c = meta[0]
    x = rope[...].astype(f32)
    lo, hi = x[:, :32], x[:, 32:]
    rot = jnp.concatenate(
        [lo * cosine[...] - hi * sine[...], hi * cosine[...] + lo * sine[...]], axis=1
    ).astype(bf16)
    rot_out[...] = rot
    for i in range(2):
        packed = jnp.concatenate([rot[i * 64 : i * 64 + 32], rot[i * 64 + 32 : i * 64 + 64]], axis=1)
        for n in range(18):
            if n < 16:
                l, r = n // 4, n % 4
                v = lat[i * 64 + r * UNIT : i * 64 + (r + 1) * UNIT, l * 128 : (l + 1) * 128]
            else:
                v = packed[(n - 16) * UNIT : (n - 15) * UNIT]
            row = i * HALF + (n % 9) * UNIT
            units[n // 9, row : row + UNIT, :] = v
    for half in range(2):
        units[half, 288:304, :] = sel[...]
    mine[...] = units[c]
    other[...] = units[1 - c]


def chip_kernel(mine, recv, x, sel):
    x[0:288] = mine[0:288]
    x[288:576] = recv[0:288]
    row = lax.broadcasted_iota(jnp.int32, (UNIT, 128), 0)
    sel[...] = jnp.where(
        row == 0, mine[288:304].astype(f32), recv[288:304].astype(f32)
    ).astype(bf16)


def line_kernel(*refs):
    for k in range(4):
        refs[4][k * 576 : (k + 1) * 576] = refs[k][...]


def pack_kernel(where_, *refs):
    ins, outs, held = refs[:4], refs[4:12], refs[12]
    for k in range(4):
        held[k * 16 : (k + 1) * 16] = ins[k][...].reshape(16, HALF, 128)
    for i in range(2):
        for k in range(4):
            for j in range(8):
                f = where_[ORDER[k] * 16 + (j // 4) * 8 + i * 4 + j % 4]
                outs[i * 4 + k][j * HALF : (j + 1) * HALF] = held[f]


def merge_kernel(i, where_, *refs):
    ins, outs, held = refs[:4], refs[4:6], refs[6]
    for k in range(4):
        held[ORDER[k] * 8 : (ORDER[k] + 1) * 8] = ins[k][...].reshape(8, HALF, 128)
    for j in range(8):
        k = where_[(j // 4) * 8 + i * 4 + j % 4]
        outs[j // 4][(j % 4) * HALF : (j % 4 + 1) * HALF] = held[k * 8 + j]


def attention_kernel(
    i, meta, lat, rot, mine, other, q_ref, qr_ref, do_ref, *refs
):
    out_ref, dkl_ref, dkr_ref, gm_ref, go_ref, units, keys, keys_r, acc, acc_r = refs[-10:]
    t = pl.program_id(0)
    c = meta[0]
    block = meta[1] + i

    @pl.when(t == 0)
    def _():
        keys[0:BLK] = lat[i * BLK : (i + 1) * BLK]
        keys_r[0:BLK] = rot[i * BLK : (i + 1) * BLK]
        units[c] = mine[...]
        units[1 - c] = other[...]
        for s in range(4):
            base = (s + 1) * BLK
            for n in range(16):
                row = s * HALF + (n % 9) * UNIT
                l, r = n // 4, n % 4
                keys[base + r * UNIT : base + (r + 1) * UNIT, l * 128 : (l + 1) * 128] = units[
                    n // 9, row : row + UNIT, :
                ]
            packed = units[1, s * HALF + 112 : s * HALF + 144, :]
            keys_r[base : base + 32] = packed[:, :64]
            keys_r[base + 32 : base + 64] = packed[:, 64:]
        acc[...] = jnp.zeros_like(acc)
        acc_r[...] = jnp.zeros_like(acc_r)

    q, qr, do = q_ref[...], qr_ref[...], do_ref[...]
    nt = (((1,), (1,)), ((), ()))
    raw = lax.dot_general(keys[...], q, nt, preferred_element_type=f32)
    raw = raw + lax.dot_general(keys_r[...], qr, nt, preferred_element_type=f32)
    key_row = lax.broadcasted_iota(jnp.int32, raw.shape, 0)
    query = lax.broadcasted_iota(jnp.int32, raw.shape, 1) // HEADS + t * (TILE // HEADS)
    limit = jnp.minimum(block + 1, SEL) * BLK
    allowed = (key_row < limit) & ((key_row >= BLK) | (key_row <= query))
    raw = jnp.where(allowed, raw, -jnp.inf)
    top = jnp.max(raw, axis=0, keepdims=True)
    expon = jnp.exp((raw - top) * softmax_scale)
    probs = expon * (1.0 / jnp.sum(expon, axis=0, keepdims=True))
    probs_low = probs.astype(bf16)
    dprobs = lax.dot_general(keys[...], do, nt, preferred_element_type=f32)
    row_delta = jnp.sum(probs * dprobs, axis=0, keepdims=True)
    dscores = (probs * (dprobs - row_delta) * softmax_scale).astype(bf16)
    out_ref[...] = lax.dot_general(
        probs_low, keys[...], (((0,), (0,)), ((), ())), preferred_element_type=f32
    ).astype(bf16)
    acc[...] += jnp.dot(dscores, q, preferred_element_type=f32) + jnp.dot(
        probs_low, do, preferred_element_type=f32
    )
    acc_r[...] += jnp.dot(dscores, qr, preferred_element_type=f32)

    @pl.when(t == pl.num_programs(0) - 1)
    def _():
        dkl_ref[...] = acc[0:BLK]
        dkr_ref[...] = acc_r[0:BLK]
        for s in range(4):
            base = (s + 1) * BLK
            packed = jnp.concatenate(
                [acc_r[base : base + 32, :], acc_r[base + 32 : base + 64, :]], axis=1
            )
            for n in range(18):
                m = n % 9
                if n < 16:
                    l, r = n // 4, n % 4
                    v = acc[base + r * UNIT : base + (r + 1) * UNIT, l * 128 : (l + 1) * 128]
                else:
                    v = packed[(n - 16) * UNIT : (n - 15) * UNIT]
                row = s * HALF + m * UNIT
                units[n // 9, row : row + UNIT, :] = v.astype(bf16)
        gm_ref[...] = units[c]
        go_ref[...] = units[1 - c]


def attention(i, meta, lat, rot, mine, other, q, qr, do, out):
    tiles = BLK * HEADS // TILE
    whole = lambda shape: pl.BlockSpec(shape, lambda t: (0, 0))
    rows = lambda width: pl.BlockSpec((TILE, width), lambda t: (i * tiles + t, 0))
    ins = [meta, lat, rot, mine, other, q, qr, do] + ([] if out is None else [out])
    return pl.pallas_call(
        functools.partial(attention_kernel, i),
        grid=(tiles,),
        out_shape=[
            jax.ShapeDtypeStruct(q.shape, bf16),
            jax.ShapeDtypeStruct((BLK, LAT), f32),
            jax.ShapeDtypeStruct((BLK, ROPE), f32),
            jax.ShapeDtypeStruct((4 * HALF, 128), bf16),
            jax.ShapeDtypeStruct((4 * HALF, 128), bf16),
        ],
        in_specs=[
            SMEM,
            whole((128, LAT)),
            whole((128, ROPE)),
            whole((4 * HALF, 128)),
            whole((4 * HALF, 128)),
            rows(LAT),
            rows(ROPE),
            rows(LAT),
        ]
        + ([] if out is None else [pl.BlockSpec(memory_space=pl.ANY)]),
        out_specs=[
            rows(LAT),
            whole((BLK, LAT)),
            whole((BLK, ROPE)),
            whole((4 * HALF, 128)),
            whole((4 * HALF, 128)),
        ],
        scratch_shapes=[
            pltpu.VMEM((2, 4 * HALF, 128), bf16),
            pltpu.VMEM((SEL * BLK, LAT), bf16),
            pltpu.VMEM((SEL * BLK, ROPE), bf16),
            pltpu.VMEM((SEL * BLK, LAT), f32),
            pltpu.VMEM((SEL * BLK, ROPE), f32),
        ],
        input_output_aliases={} if out is None else {8: 0},
        compiler_params=pltpu.CompilerParams(vmem_limit_bytes=58 * 1024 * 1024),
        cost_estimate=pl.CostEstimate(flops=1000, bytes_accessed=1000, transcendentals=0),
        name="attention",
    )(*ins)


def slots_kernel(mine, recv, g):
    g[0:576] = mine[...]
    g[576:1152] = recv[...]


def plane_kernel(where_, *refs):
    ins, outs, acc = refs[:8], refs[8:12], refs[12]
    acc[...] = jnp.zeros_like(acc)
    for i in range(2):
        for k in range(4):
            for j in range(8):
                f = where_[k * 16 + (j // 4) * 8 + i * 4 + j % 4]
                acc[f] = acc[f] + ins[i * 4 + k][j * HALF : (j + 1) * HALF].astype(f32)
    for k in range(4):
        for j in range(16):
            outs[k][j * HALF : (j + 1) * HALF] = acc[ORDER[k] * 16 + j].astype(outs[k].dtype)


def sum_rows(ins, at):
    total = ins[0][at : at + HALF]
    for k in range(1, 4):
        total = total + ins[k][at : at + HALF].astype(f32)
    return total


def column_kernel(*refs):
    ins, outs = refs[:4], refs[4:8]
    for j in range(16):
        out, row = outs[ORDER.index(j // 4)], (j % 4) * HALF
        out[row : row + HALF] = sum_rows(ins, j * HALF).astype(out.dtype)


def owner_kernel(*refs):
    ins, outs = refs[:4], refs[4:6]
    for j in range(4):
        row = (j % 2) * HALF
        outs[j // 2][row : row + HALF] = sum_rows(ins, j * HALF)


def half_sum_kernel(meta, mine, recv, dkl0, dkl1, dkr0, dkr1, out, units):
    c = meta[0]
    units[c] = mine[...]
    units[1 - c] = recv[...]
    for i in range(2):
        dkl, dkr = (dkl0, dkl1)[i], (dkr0, dkr1)[i]
        packed = jnp.concatenate([dkr[0:32], dkr[32:64]], axis=1)
        for n in range(18):
            if n < 16:
                l, r = n // 4, n % 4
                own = dkl[r * UNIT : (r + 1) * UNIT, l * 128 : (l + 1) * 128]
            else:
                own = packed[(n - 16) * UNIT : (n - 15) * UNIT]
            row = i * HALF + (n % 9) * UNIT
            to = (i * 18 + n) * UNIT
            out[to : to + UNIT] = (units[n // 9, row : row + UNIT, :] + own).astype(bf16)


def final_kernel(mine, recv, cosine, sine, lat_out, rope_out):
    for i in range(2):
        for n in range(16):
            l, r = n // 4, n % 4
            at = (i * 18 + n) * UNIT
            lat_out[i * 64 + r * UNIT : i * 64 + (r + 1) * UNIT, l * 128 : (l + 1) * 128] = mine[
                at : at + UNIT
            ].astype(f32) + recv[at : at + UNIT].astype(f32)
        at = (i * 18 + 16) * UNIT
        packed = mine[at : at + 32].astype(f32) + recv[at : at + 32].astype(f32)
        for part in range(2):
            rows = slice(i * 64 + part * 32, i * 64 + part * 32 + 32)
            g = packed[:, part * 64 : part * 64 + 64]
            lo, hi = g[:, :32], g[:, 32:]
            cs, sn = cosine[rows, :], sine[rows, :]
            rope_out[rows, :] = jnp.concatenate([lo * cs + hi * sn, hi * cs - lo * sn], axis=1)


def shards(latent, rope_key, queries, query_rope, grad_out, sel_blocks):
    x, y, z, c = [lax.axis_index(a) for a in "xyzc"]
    ctx = ((x * 4 + y) * 4 + z) * 2 + c
    meta = jnp.stack([c, ctx * 2]).astype(jnp.int32)

    positions = ctx * 128 + jnp.arange(128, dtype=jnp.int32)
    freq_steps = jnp.arange(ROPE // 2, dtype=f32)
    inverse_freq = rope_base ** (-2.0 * freq_steps / ROPE)
    angles = positions.astype(f32)[:, None] * inverse_freq[None, :]
    cosine, sine = jnp.cos(angles), jnp.sin(angles)

    sel_row = sel_blocks[:, 1:].reshape(1, 8).astype(bf16)
    sel_unit = jnp.broadcast_to(jnp.pad(sel_row, ((0, 0), (0, 120))), (UNIT, 128))
    mine, other, rot = call(
        prep_kernel,
        (meta, latent, rope_key, cosine, sine, sel_unit),
        [((304, 128), bf16), ((304, 128), bf16), ((128, ROPE), bf16)],
        [pltpu.VMEM((2, 304, 128), bf16)],
        scalars=1,
        name="prep",
    )
    chip, sel = call(
        chip_kernel, (mine, swap(other, "c")), [((576, 128), bf16), ((UNIT, 128), bf16)], name="chip"
    )

    def each_of(parts, phase):
        return [parts[0]] + [exchange(part, phase, k) for part, k in zip(parts[1:], ORDER[1:])]

    def all_of(a, phase):
        return [a] + [exchange(a, phase, k) for k in DISTANCES]

    qr, chip = lax.optimization_barrier((query_rope.reshape(128 * HEADS, ROPE), chip))
    lines = all_of(chip, "u")
    (line,) = call(line_kernel, lines, [((2304, 128), bf16)], name="line")
    planes = all_of(line, "v")

    asked = jnp.stack([t[:2, :8] for t in all_of(sel, "w")]).astype(jnp.int32).reshape(4, 16)
    sx, sy, sz = asked >> 6, (asked >> 4) & 3, (asked >> 2) & 3
    local = jnp.where(((asked >> 1) & 1) == c, 0, 2) + (asked & 1)
    on_v = jnp.where(c == 0, x ^ sx, y ^ sy)
    on_w = jnp.where(c == 0, y ^ sy, x ^ sx)
    pos = on_v * 16 + (z ^ sz) * 4 + local
    pack_at = pos.reshape(-1)
    add_at = jnp.where(on_w == 0, pos, 64).reshape(-1)
    merge_at = on_w[0]

    q = queries.reshape(128 * HEADS, LAT)
    do = grad_out.reshape(128 * HEADS, LAT)
    packed = call(
        pack_kernel,
        [pack_at] + planes,
        [((8 * HALF, 128), bf16)] * 8,
        [pltpu.VMEM((64, HALF, 128), bf16)],
        scalars=1,
        name="pack",
    )
    got = [each_of(packed[i * 4 : i * 4 + 4], "w") for i in range(2)]
    out, own_grads, grads = None, [], []
    for i in range(2):
        key_mine, key_other = call(
            functools.partial(merge_kernel, i),
            [merge_at] + got[i],
            [((4 * HALF, 128), bf16)] * 2,
            [pltpu.VMEM((32, HALF, 128), bf16)],
            scalars=1,
            name="merge",
        )
        key_recv = swap(key_other, "c")
        out, dkl, dkr, g_mine, g_other = attention(
            i, meta, latent, rot, key_mine, key_recv, q, qr, do, out
        )
        g_recv = swap(g_other, "c")
        if grads:
            *grads, g_recv = lax.optimization_barrier((*grads, g_recv))
        (slots,) = call(slots_kernel, (g_mine, g_recv), [((8 * HALF, 128), bf16)], name="slots")
        own_grads.append((dkl, dkr))
        grads += all_of(slots, "w")
        merge_at, meta, _ = lax.optimization_barrier((merge_at, meta, slots))
    sums = call(
        plane_kernel,
        [add_at] + grads,
        [((2304, 128), bf16 if k else f32) for k in range(4)],
        [pltpu.VMEM((65, HALF, 128), f32)],
        scalars=1,
        name="plane",
    )
    got = each_of(sums, "v")
    sums = call(column_kernel, got, [((576, 128), bf16 if k else f32) for k in range(4)], name="column")
    got = each_of(sums, "u")
    f_mine, f_other = call(owner_kernel, got, [((288, 128), f32)] * 2, name="owner")
    (total,) = call(
        half_sum_kernel,
        (meta, f_mine, swap(f_other, "c"), own_grads[0][0], own_grads[1][0], own_grads[0][1], own_grads[1][1]),
        [((576, 128), bf16)],
        [pltpu.VMEM((2, 288, 128), f32)],
        scalars=1,
        name="half_sum",
    )
    d_latent, d_rope_key = call(
        final_kernel,
        (total, swap(total, "h"), cosine, sine),
        [((128, LAT), f32), ((128, ROPE), f32)],
        name="final",
    )
    return out.reshape(128, HEADS, LAT), d_latent, d_rope_key


def solution(mesh):
    lines = Mesh(mesh.devices.reshape(4, 4, 4, 2, 2), MESH)
    ctx = ("x", "y", "z", "c")
    return jax.shard_map(
        shards,
        mesh=lines,
        in_specs=(
            P(ctx, None),
            P(ctx, None),
            P(ctx, "h", None),
            P(ctx, "h"),
            P(ctx, "h", None),
            P(ctx, None),
        ),
        out_specs=(P(ctx, "h", None), P(ctx, None), P(ctx, None)),
        check_vma=False,
    )
```

```python
import functools

import jax
import jax.numpy as jnp
from jax import lax
from jax.experimental import pallas as pl
from jax.experimental.pallas import tpu as pltpu
from jax.sharding import Mesh, PartitionSpec as P

BLK = 64
SEL = 5
LAT = 512
ROPE = 64
HEADS = 32
UNIT = 16
HALF = 144
TILE = 1024
ORDER = (0, 3, 2, 1)

softmax_scale = 192.0 ** (-0.5)
rope_base = 10000.0
log2_e = 1.4426950408889634

bf16 = jnp.bfloat16
f32 = jnp.float32
VMEM = pl.BlockSpec(memory_space=pltpu.VMEM)
SMEM = pl.BlockSpec(memory_space=pltpu.SMEM)
PARAMS = pltpu.CompilerParams(vmem_limit_bytes=48 * 1024 * 1024)


def call(kernel, ins, outs, scratch=(), scalars=0, name=None):
    specs = [SMEM] * scalars + [VMEM] * (len(ins) - scalars)
    return pl.pallas_call(
        kernel,
        out_shape=[jax.ShapeDtypeStruct(s, d) for s, d in outs],
        in_specs=specs,
        out_specs=[VMEM] * len(outs),
        scratch_shapes=list(scratch),
        compiler_params=PARAMS,
        name=name,
    )(*ins)


MESH = ("x", "y", "z", "c", "h")


def partner(place, phase, k):
    x, y, z, c, h = place
    axis = "z" if phase == "u" else "xy"[c if phase == "v" else 1 - c]
    if axis == "x":
        x ^= k
    elif axis == "y":
        y ^= k
    else:
        ring = h * 4 + z
        if k == 3:
            ring = (ring + (1 if ring % 2 else 7)) % 8
        else:
            ring ^= k
        h, z = ring // 4, ring % 4
    return x, y, z, c, h


def number(place):
    x, y, z, c, h = place
    return (((x * 4 + y) * 4 + z) * 2 + c) * 2 + h


def exchange(a, phase, k):
    places = [(i // 64, i // 16 % 4, i // 4 % 4, i // 2 % 2, i % 2) for i in range(256)]
    return lax.ppermute(a, MESH, [(number(p), number(partner(p, phase, k))) for p in places])


def swap(a, axis):
    return lax.ppermute(a, axis, [(0, 1), (1, 0)])


def prep_kernel(meta, lat, rope, cosine, sine, sel, mine, other, rot_out, units):
    c = meta[0]
    x = rope[...].astype(f32)
    lo, hi = x[:32], x[32:]
    rot = jnp.concatenate(
        [lo * cosine[...] - hi * sine[...], hi * cosine[...] + lo * sine[...]], axis=0
    ).T.astype(bf16)
    rot_out[...] = rot
    for i in range(2):
        packed = jnp.concatenate([rot[i * 64 : i * 64 + 32], rot[i * 64 + 32 : i * 64 + 64]], axis=1)
        for n in range(18):
            if n < 16:
                l, r = n // 4, n % 4
                v = lat[i * 64 + r * UNIT : i * 64 + (r + 1) * UNIT, l * 128 : (l + 1) * 128]
            else:
                v = packed[(n - 16) * UNIT : (n - 15) * UNIT]
            row = i * HALF + (n % 9) * UNIT
            units[n // 9, row : row + UNIT, :] = v
    for half in range(2):
        units[half, 288:304, :] = sel[...]
    mine[...] = units[c]
    other[...] = units[1 - c]


def chip_kernel(mine, recv, x, sel):
    x[0:288] = mine[0:288]
    x[288:576] = recv[0:288]
    row = lax.broadcasted_iota(jnp.int32, (UNIT, 128), 0)
    sel[...] = jnp.where(
        row == 0, mine[288:304].astype(f32), recv[288:304].astype(f32)
    ).astype(bf16)


def line_kernel(*refs):
    for k in range(3):
        refs[3][k * 576 : (k + 1) * 576] = refs[k][...]


def pack_kernel(where_, *refs):
    own, rest, outs, held = refs[:4], refs[4:8], refs[8:12], refs[12]
    for k in range(4):
        held[k * 16 : k * 16 + 4] = own[k][...].reshape(4, HALF, 128)
        held[k * 16 + 4 : k * 16 + 16] = rest[k][...].reshape(12, HALF, 128)
    for k in range(4):
        for s in range(16):
            outs[k][s * HALF : (s + 1) * HALF] = held[where_[ORDER[k] * 16 + s]]


def merge_kernel(where_, *refs):
    ins, mine, other, held = refs[:4], refs[4], refs[5], refs[6]
    for k in range(4):
        held[ORDER[k] * 16 : (ORDER[k] + 1) * 16] = ins[k][...].reshape(16, HALF, 128)
    for s in range(16):
        out = mine if s < 8 else other
        row = (s % 8) * HALF
        out[row : row + HALF] = held[where_[s] * 16 + s]


def attention_kernel(
    meta, lat, rot, mine, other, q_ref, qr_ref, do_ref,
    out_ref, dkl_ref, dkr_ref, gm_ref, go_ref,
    units, keys, keys_r, acc, acc_r,
):
    i, t = pl.program_id(0), pl.program_id(1)
    c = meta[0]
    block = meta[1] + i

    @pl.when(t == 0)
    def _():
        rows = pl.ds(pl.multiple_of(i * BLK, BLK), BLK)
        keys[0:BLK] = lat[rows, :]
        keys_r[0:BLK] = rot[rows, :]
        part = pl.ds(pl.multiple_of(i * 576, 576), 576)
        units[c] = mine[part, :]
        units[1 - c] = other[part, :]
        for s in range(4):
            base = (s + 1) * BLK
            for n in range(16):
                row = s * HALF + (n % 9) * UNIT
                l, r = n // 4, n % 4
                keys[base + r * UNIT : base + (r + 1) * UNIT, l * 128 : (l + 1) * 128] = units[
                    n // 9, row : row + UNIT, :
                ]
            packed = units[1, s * HALF + 112 : s * HALF + 144, :]
            keys_r[base : base + 32] = packed[:, :64]
            keys_r[base + 32 : base + 64] = packed[:, 64:]
        acc[...] = jnp.zeros_like(acc)
        acc_r[...] = jnp.zeros_like(acc_r)

    nt = (((1,), (1,)), ((), ()))
    limit = jnp.minimum(block + 1, SEL) * BLK
    part = TILE // 4
    grad = jnp.zeros((SEL * BLK, LAT), f32)
    grad_r = jnp.zeros((SEL * BLK, ROPE), f32)
    raws, dps = [], []
    for j in range(4):
        rows = slice(j * part, (j + 1) * part)
        q, qr, do = q_ref[rows, :], qr_ref[rows, :], do_ref[rows, :]
        raw = lax.dot_general(keys[...], q, nt, preferred_element_type=f32)
        raw = raw + lax.dot_general(keys_r[...], qr, nt, preferred_element_type=f32)
        raws.append(raw)
        dps.append(lax.dot_general(keys[...], do, nt, preferred_element_type=f32))
    for j in range(4):
        rows = slice(j * part, (j + 1) * part)
        q, qr, do = q_ref[rows, :], qr_ref[rows, :], do_ref[rows, :]
        raw, dprobs = raws[j], dps[j]
        key_row = lax.broadcasted_iota(jnp.int32, (BLK, part), 0)
        query = lax.broadcasted_iota(jnp.int32, (BLK, part), 1) // HEADS + t * (TILE // HEADS) + j * (part // HEADS)
        bands = [jnp.where(key_row <= query, raw[:BLK], -jnp.inf)]
        for s in range(1, SEL):
            bands.append(raw[s * BLK : (s + 1) * BLK] + jnp.where(s * BLK < limit, 0.0, -jnp.inf))
        raw = jnp.concatenate(bands, axis=0)
        top = jnp.max(raw, axis=0, keepdims=True)
        expon = jnp.exp2((raw - top) * (softmax_scale * log2_e))
        probs = expon * (1.0 / jnp.sum(expon, axis=0, keepdims=True))
        probs_low = probs.astype(bf16)
        row_delta = jnp.sum(probs * dprobs, axis=0, keepdims=True)
        dscores = (probs * ((dprobs - row_delta) * softmax_scale)).astype(bf16)
        out_ref[rows, :] = lax.dot_general(
            probs_low, keys[...], (((0,), (0,)), ((), ())), preferred_element_type=f32
        ).astype(bf16)
        grad = grad + jnp.dot(dscores, q, preferred_element_type=f32) + jnp.dot(probs_low, do, preferred_element_type=f32)
        grad_r = grad_r + jnp.dot(dscores, qr, preferred_element_type=f32)
    acc[...] += grad
    acc_r[...] += grad_r

    @pl.when(t == pl.num_programs(1) - 1)
    def _():
        rows = pl.ds(pl.multiple_of(i * BLK, BLK), BLK)
        dkl_ref[rows, :] = acc[0:BLK]
        dkr_ref[rows, :] = acc_r[0:BLK]
        for s in range(4):
            base = (s + 1) * BLK
            packed = jnp.concatenate(
                [acc_r[base : base + 32, :], acc_r[base + 32 : base + 64, :]], axis=1
            )
            for n in range(18):
                m = n % 9
                if n < 16:
                    l, r = n // 4, n % 4
                    v = acc[base + r * UNIT : base + (r + 1) * UNIT, l * 128 : (l + 1) * 128]
                else:
                    v = packed[(n - 16) * UNIT : (n - 15) * UNIT]
                row = s * HALF + m * UNIT
                units[n // 9, row : row + UNIT, :] = v.astype(bf16)
        part = pl.ds(pl.multiple_of(i * 576, 576), 576)
        gm_ref[part, :] = units[c]
        go_ref[part, :] = units[1 - c]


def attention(meta, lat, rot, mine, other, q, qr, do):
    tiles = BLK * HEADS // TILE
    whole = lambda shape: pl.BlockSpec(shape, lambda i, t: (0, 0))
    rows = lambda width: pl.BlockSpec((TILE, width), lambda i, t: (i * tiles + t, 0))
    return pl.pallas_call(
        attention_kernel,
        grid=(2, tiles),
        out_shape=[
            jax.ShapeDtypeStruct(q.shape, bf16),
            jax.ShapeDtypeStruct((128, LAT), f32),
            jax.ShapeDtypeStruct((128, ROPE), f32),
            jax.ShapeDtypeStruct((8 * HALF, 128), bf16),
            jax.ShapeDtypeStruct((8 * HALF, 128), bf16),
        ],
        in_specs=[
            SMEM,
            whole((128, LAT)),
            whole((128, ROPE)),
            whole((8 * HALF, 128)),
            whole((8 * HALF, 128)),
            rows(LAT),
            rows(ROPE),
            rows(LAT),
        ],
        out_specs=[
            rows(LAT),
            whole((128, LAT)),
            whole((128, ROPE)),
            whole((8 * HALF, 128)),
            whole((8 * HALF, 128)),
        ],
        scratch_shapes=[
            pltpu.VMEM((2, 576, 128), bf16),
            pltpu.VMEM((SEL * BLK, LAT), bf16),
            pltpu.VMEM((SEL * BLK, ROPE), bf16),
            pltpu.VMEM((SEL * BLK, LAT), f32),
            pltpu.VMEM((SEL * BLK, ROPE), f32),
        ],
        compiler_params=PARAMS,
        name="attention",
    )(meta, lat, rot, mine, other, q, qr, do)


def slots_kernel(mine, recv, g):
    g[0:1152] = mine[...]
    g[1152:2304] = recv[...]


def plane_kernel(where_, *refs):
    ins, rest, own, acc = refs[:4], refs[4:8], refs[8:12], refs[12]
    acc[...] = jnp.zeros_like(acc)
    for k in range(4):
        for s in range(16):
            f = where_[k * 16 + s]
            acc[f] = acc[f] + ins[k][s * HALF : (s + 1) * HALF].astype(f32)
    for k in range(4):
        for j in range(16):
            out, row = (own[k], j) if j < 4 else (rest[k], j - 4)
            out[row * HALF : (row + 1) * HALF] = acc[ORDER[k] * 16 + j].astype(out.dtype)


def sum_rows(ins, at):
    total = ins[0][at : at + HALF].astype(f32)
    for part in ins[1:]:
        total = total + part[at : at + HALF].astype(f32)
    return total


def column_kernel(*refs):
    ins, outs = refs[:4], refs[4:7]
    for j in range(12):
        out, row = outs[ORDER.index(j // 4 + 1) - 1], (j % 4) * HALF
        out[row : row + HALF] = sum_rows(ins, j * HALF).astype(bf16)


def owner_kernel(*refs):
    ins, outs = refs[:7], refs[7:9]
    for j in range(4):
        row = (j % 2) * HALF
        outs[j // 2][row : row + HALF] = sum_rows(ins, j * HALF)


def half_sum_kernel(meta, mine, recv, dkl, dkr, out, units):
    c = meta[0]
    units[c] = mine[...]
    units[1 - c] = recv[...]
    for i in range(2):
        lo, hi = slice(i * 64, i * 64 + 32), slice(i * 64 + 32, i * 64 + 64)
        packed = jnp.concatenate([dkr[lo, :], dkr[hi, :]], axis=1)
        for n in range(18):
            if n < 16:
                l, r = n // 4, n % 4
                own = dkl[i * 64 + r * UNIT : i * 64 + (r + 1) * UNIT, l * 128 : (l + 1) * 128]
            else:
                own = packed[(n - 16) * UNIT : (n - 15) * UNIT]
            row = i * HALF + (n % 9) * UNIT
            to = (i * 18 + n) * UNIT
            out[to : to + UNIT] = (units[n // 9, row : row + UNIT, :] + own).astype(bf16)


def final_kernel(mine, recv, cosine, sine, lat_out, rope_out):
    parts = []
    for i in range(2):
        for n in range(16):
            l, r = n // 4, n % 4
            at = (i * 18 + n) * UNIT
            lat_out[i * 64 + r * UNIT : i * 64 + (r + 1) * UNIT, l * 128 : (l + 1) * 128] = mine[
                at : at + UNIT
            ].astype(f32) + recv[at : at + UNIT].astype(f32)
        at = (i * 18 + 16) * UNIT
        packed = mine[at : at + 32].astype(f32) + recv[at : at + 32].astype(f32)
        parts += [packed[:, :64], packed[:, 64:]]
    g = jnp.concatenate(parts, axis=0).T
    lo, hi, cs, sn = g[:32], g[32:], cosine[...], sine[...]
    rope_out[...] = jnp.concatenate([lo * cs + hi * sn, hi * cs - lo * sn], axis=0)


def shards(latent, rope_key, queries, query_rope, grad_out, sel_blocks):
    x, y, z, c = [lax.axis_index(a) for a in "xyzc"]
    ctx = ((x * 4 + y) * 4 + z) * 2 + c
    meta = jnp.stack([c, ctx * 2]).astype(jnp.int32)

    positions = ctx * 128 + jnp.arange(128, dtype=jnp.int32)
    freq_steps = jnp.arange(ROPE // 2, dtype=f32)
    inverse_freq = rope_base ** (-2.0 * freq_steps / ROPE)
    angles = positions.astype(f32)[None, :] * inverse_freq[:, None]
    cosine, sine = jnp.cos(angles), jnp.sin(angles)

    sel_row = sel_blocks[:, 1:].reshape(1, 8).astype(bf16)
    sel_unit = jnp.broadcast_to(jnp.pad(sel_row, ((0, 0), (0, 120))), (UNIT, 128))
    mine, other, rot = call(
        prep_kernel,
        (meta, latent, rope_key.T, cosine, sine, sel_unit),
        [((304, 128), bf16), ((304, 128), bf16), ((128, ROPE), bf16)],
        [pltpu.VMEM((2, 304, 128), bf16)],
        scalars=1,
        name="prep",
    )
    chip, sel = call(
        chip_kernel, (mine, swap(other, "c")), [((576, 128), bf16), ((UNIT, 128), bf16)], name="chip"
    )

    def all_of(a, phase):
        return [a] + [exchange(a, phase, k) for k in (1, 2, 3)]

    def each_of(parts, phase):
        return [exchange(part, phase, k) for part, k in zip(parts, ORDER[1:])]

    own_plane = all_of(chip, "v")
    lines = all_of(chip, "u")
    got = lax.optimization_barrier((*own_plane[1:], *lines[1:]))
    own_plane = [chip, *got[:3]]
    (line,) = call(line_kernel, got[3:], [((1728, 128), bf16)], name="line")
    rest_plane = all_of(line, "v")

    asked = jnp.stack([t[:2, :8] for t in all_of(sel, "w")]).astype(jnp.int32).reshape(4, 16)
    sx, sy, sz = asked >> 6, (asked >> 4) & 3, (asked >> 2) & 3
    local = jnp.where(((asked >> 1) & 1) == c, 0, 2) + (asked & 1)
    on_v = jnp.where(c == 0, x ^ sx, y ^ sy)
    on_w = jnp.where(c == 0, y ^ sy, x ^ sx)
    pos = on_v * 16 + (z ^ sz) * 4 + local
    pack_at = pos.reshape(-1)
    add_at = jnp.where(on_w == 0, pos, 64).reshape(-1)
    merge_at = on_w[0]

    packed = call(
        pack_kernel,
        [pack_at] + own_plane + rest_plane,
        [((2304, 128), bf16)] * 4,
        [pltpu.VMEM((64, HALF, 128), bf16)],
        scalars=1,
        name="pack",
    )
    got = [packed[0]] + each_of(packed[1:], "w")
    key_mine, key_other = call(
        merge_kernel,
        [merge_at] + got,
        [((8 * HALF, 128), bf16)] * 2,
        [pltpu.VMEM((64, HALF, 128), bf16)],
        scalars=1,
        name="merge",
    )
    key_recv = swap(key_other, "c")

    q = queries.reshape(128 * HEADS, LAT)
    do = grad_out.reshape(128 * HEADS, LAT)
    qr = query_rope.reshape(128 * HEADS, ROPE)
    out, dkl, dkr, g_mine, g_other = attention(meta, latent, rot, key_mine, key_recv, q, qr, do)

    (slots,) = call(slots_kernel, (g_mine, swap(g_other, "c")), [((2304, 128), bf16)], name="slots")
    sums = call(
        plane_kernel,
        [add_at] + all_of(slots, "w"),
        [((rows, 128), bf16 if k else f32) for rows in (1728, 576) for k in range(4)],
        [pltpu.VMEM((65, HALF, 128), f32)],
        scalars=1,
        name="plane",
    )
    rest, own = sums[:4], sums[4:]
    columns = call(
        column_kernel, [rest[0]] + each_of(rest[1:], "v"), [((576, 128), bf16)] * 3, name="column"
    )
    got = [own[0]] + each_of(own[1:], "v") + each_of(columns, "u")
    f_mine, f_other = call(owner_kernel, got, [((288, 128), f32)] * 2, name="owner")
    (total,) = call(
        half_sum_kernel,
        (meta, f_mine, swap(f_other, "c"), dkl, dkr),
        [((576, 128), bf16)],
        [pltpu.VMEM((2, 288, 128), f32)],
        scalars=1,
        name="half_sum",
    )
    d_latent, d_rope_key = call(
        final_kernel,
        (total, swap(total, "h"), cosine, sine),
        [((128, LAT), f32), ((ROPE, 128), f32)],
        name="final",
    )
    return out.reshape(128, HEADS, LAT), d_latent, d_rope_key.T


def solution(mesh):
    lines = Mesh(mesh.devices.reshape(4, 4, 4, 2, 2), MESH)
    ctx = ("x", "y", "z", "c")
    return jax.shard_map(
        shards,
        mesh=lines,
        in_specs=(
            P(ctx, None),
            P(ctx, None),
            P(ctx, "h", None),
            P(ctx, "h"),
            P(ctx, "h", None),
            P(ctx, None),
        ),
        out_specs=(P(ctx, "h", None), P(ctx, None), P(ctx, None)),
        check_vma=False,
    )
```

```python
import functools

import jax
import jax.numpy as jnp
from jax import lax
from jax.experimental import pallas as pl
from jax.experimental.pallas import tpu as pltpu
from jax.sharding import Mesh, PartitionSpec as P

BLK = 64
SEL = 5
LAT = 512
ROPE = 64
HEADS = 32
UNIT = 16
HALF = 144
TILE = 1024
ORDER = (0, 3, 2, 1)

softmax_scale = 192.0 ** (-0.5)
rope_base = 10000.0
log2_e = 1.4426950408889634

bf16 = jnp.bfloat16
f32 = jnp.float32
VMEM = pl.BlockSpec(memory_space=pltpu.VMEM)
SMEM = pl.BlockSpec(memory_space=pltpu.SMEM)
PARAMS = pltpu.CompilerParams(vmem_limit_bytes=48 * 1024 * 1024)


def call(kernel, ins, outs, scratch=(), scalars=0, name=None):
    specs = [SMEM] * scalars + [VMEM] * (len(ins) - scalars)
    return pl.pallas_call(
        kernel,
        out_shape=[jax.ShapeDtypeStruct(s, d) for s, d in outs],
        in_specs=specs,
        out_specs=[VMEM] * len(outs),
        scratch_shapes=list(scratch),
        compiler_params=PARAMS,
        name=name,
    )(*ins)


MESH = ("x", "y", "z", "c", "h")


def partner(place, phase, k):
    x, y, z, c, h = place
    axis = "z" if phase == "u" else "xy"[c if phase == "v" else 1 - c]
    if axis == "x":
        x ^= k
    elif axis == "y":
        y ^= k
    else:
        ring = h * 4 + z
        if k == 3:
            ring = (ring + (1 if ring % 2 else 7)) % 8
        else:
            ring ^= k
        h, z = ring // 4, ring % 4
    return x, y, z, c, h


def number(place):
    x, y, z, c, h = place
    return (((x * 4 + y) * 4 + z) * 2 + c) * 2 + h


def exchange(a, phase, k):
    places = [(i // 64, i // 16 % 4, i // 4 % 4, i // 2 % 2, i % 2) for i in range(256)]
    return lax.ppermute(a, MESH, [(number(p), number(partner(p, phase, k))) for p in places])


def swap(a, axis):
    return lax.ppermute(a, axis, [(0, 1), (1, 0)])


def prep_kernel(meta, lat, rope, cosine, sine, sel, mine, other, rot_out, units):
    c = meta[0]
    x = rope[...].astype(f32)
    lo, hi = x[:32], x[32:]
    rot = jnp.concatenate(
        [lo * cosine[...] - hi * sine[...], hi * cosine[...] + lo * sine[...]], axis=0
    ).T.astype(bf16)
    rot_out[...] = rot
    for i in range(2):
        packed = jnp.concatenate([rot[i * 64 : i * 64 + 32], rot[i * 64 + 32 : i * 64 + 64]], axis=1)
        for n in range(18):
            if n < 16:
                l, r = n // 4, n % 4
                v = lat[i * 64 + r * UNIT : i * 64 + (r + 1) * UNIT, l * 128 : (l + 1) * 128]
            else:
                v = packed[(n - 16) * UNIT : (n - 15) * UNIT]
            row = i * HALF + (n % 9) * UNIT
            units[n // 9, row : row + UNIT, :] = v
    for half in range(2):
        units[half, 288:304, :] = sel[...]
    mine[...] = units[c]
    other[...] = units[1 - c]


def chip_kernel(mine, recv, x, sel):
    x[0:288] = mine[0:288]
    x[288:576] = recv[0:288]
    row = lax.broadcasted_iota(jnp.int32, (UNIT, 128), 0)
    sel[...] = jnp.where(
        row == 0, mine[288:304].astype(f32), recv[288:304].astype(f32)
    ).astype(bf16)


def line_kernel(*refs):
    for k in range(3):
        refs[3][k * 576 : (k + 1) * 576] = refs[k][...]


def pack_kernel(where_, *refs):
    own, rest, outs, held = refs[:4], refs[4:8], refs[8:12], refs[12]
    for k in range(4):
        held[k * 16 : k * 16 + 4] = own[k][...].reshape(4, HALF, 128)
        held[k * 16 + 4 : k * 16 + 16] = rest[k][...].reshape(12, HALF, 128)
    for k in range(4):
        for s in range(16):
            outs[k][s * HALF : (s + 1) * HALF] = held[where_[ORDER[k] * 16 + s]]


def merge_kernel(where_, *refs):
    ins, mine, other, held = refs[:4], refs[4], refs[5], refs[6]
    for k in range(4):
        held[ORDER[k] * 16 : (ORDER[k] + 1) * 16] = ins[k][...].reshape(16, HALF, 128)
    for s in range(16):
        out = mine if s < 8 else other
        row = (s % 8) * HALF
        out[row : row + HALF] = held[where_[s] * 16 + s]


def attention_kernel(
    meta, lat, rot, mine, other, q_ref, qr_ref, do_ref,
    probs_ref, ds_ref, keys_out, gm_ref, go_ref,
    units, keys, keys_r, acc, acc_r,
):
    i, t = pl.program_id(0), pl.program_id(1)
    c = meta[0]
    block = meta[1] + i

    @pl.when(t == 0)
    def _():
        rows = pl.ds(pl.multiple_of(i * BLK, BLK), BLK)
        keys[0:BLK] = lat[rows, :]
        keys_r[0:BLK] = rot[rows, :]
        part = pl.ds(pl.multiple_of(i * 576, 576), 576)
        units[c] = mine[part, :]
        units[1 - c] = other[part, :]
        for s in range(4):
            base = (s + 1) * BLK
            for n in range(16):
                row = s * HALF + (n % 9) * UNIT
                l, r = n // 4, n % 4
                keys[base + r * UNIT : base + (r + 1) * UNIT, l * 128 : (l + 1) * 128] = units[
                    n // 9, row : row + UNIT, :
                ]
            packed = units[1, s * HALF + 112 : s * HALF + 144, :]
            keys_r[base : base + 32] = packed[:, :64]
            keys_r[base + 32 : base + 64] = packed[:, 64:]
        keys_out[...] = keys[...]
        acc[...] = jnp.zeros_like(acc)
        acc_r[...] = jnp.zeros_like(acc_r)

    nt = (((1,), (1,)), ((), ()))
    limit = jnp.minimum(block + 1, SEL) * BLK
    part = TILE // 4
    grad = jnp.zeros(((SEL - 1) * BLK, LAT), f32)
    grad_r = jnp.zeros(((SEL - 1) * BLK, ROPE), f32)
    raws, dps = [], []
    for j in range(4):
        rows = slice(j * part, (j + 1) * part)
        q, qr, do = q_ref[rows, :], qr_ref[rows, :], do_ref[rows, :]
        raw = lax.dot_general(keys[...], q, nt, preferred_element_type=f32)
        raw = raw + lax.dot_general(keys_r[...], qr, nt, preferred_element_type=f32)
        raws.append(raw)
        dps.append(lax.dot_general(keys[...], do, nt, preferred_element_type=f32))
    for j in range(4):
        rows = slice(j * part, (j + 1) * part)
        q, qr, do = q_ref[rows, :], qr_ref[rows, :], do_ref[rows, :]
        raw, dprobs = raws[j], dps[j]
        key_row = lax.broadcasted_iota(jnp.int32, (BLK, part), 0)
        query = lax.broadcasted_iota(jnp.int32, (BLK, part), 1) // HEADS + t * (TILE // HEADS) + j * (part // HEADS)
        bands = [jnp.where(key_row <= query, raw[:BLK], -jnp.inf)]
        for s in range(1, SEL):
            bands.append(raw[s * BLK : (s + 1) * BLK] + jnp.where(s * BLK < limit, 0.0, -jnp.inf))
        raw = jnp.concatenate(bands, axis=0)
        top = jnp.max(raw, axis=0, keepdims=True)
        expon = jnp.exp2((raw - top) * (softmax_scale * log2_e))
        probs = expon * (1.0 / jnp.sum(expon, axis=0, keepdims=True))
        probs_low = probs.astype(bf16)
        row_delta = jnp.sum(probs * dprobs, axis=0, keepdims=True)
        dscores = (probs * ((dprobs - row_delta) * softmax_scale)).astype(bf16)
        probs_ref[:, rows] = probs_low
        ds_ref[:, rows] = dscores[:BLK]
        grad = grad + jnp.dot(dscores[BLK:], q, preferred_element_type=f32)
        grad = grad + jnp.dot(probs_low[BLK:], do, preferred_element_type=f32)
        grad_r = grad_r + jnp.dot(dscores[BLK:], qr, preferred_element_type=f32)
    acc[...] += grad
    acc_r[...] += grad_r

    @pl.when(t == pl.num_programs(1) - 1)
    def _():
        for s in range(4):
            base = s * BLK
            packed = jnp.concatenate(
                [acc_r[base : base + 32, :], acc_r[base + 32 : base + 64, :]], axis=1
            )
            for n in range(18):
                m = n % 9
                if n < 16:
                    l, r = n // 4, n % 4
                    v = acc[base + r * UNIT : base + (r + 1) * UNIT, l * 128 : (l + 1) * 128]
                else:
                    v = packed[(n - 16) * UNIT : (n - 15) * UNIT]
                row = s * HALF + m * UNIT
                units[n // 9, row : row + UNIT, :] = v.astype(bf16)
        part = pl.ds(pl.multiple_of(i * 576, 576), 576)
        gm_ref[part, :] = units[c]
        go_ref[part, :] = units[1 - c]


def attention(meta, lat, rot, mine, other, q, qr, do):
    tiles = BLK * HEADS // TILE
    whole = lambda shape: pl.BlockSpec(shape, lambda i, t: (0, 0))
    rows = lambda width: pl.BlockSpec((TILE, width), lambda i, t: (i * tiles + t, 0))
    return pl.pallas_call(
        attention_kernel,
        grid=(2, tiles),
        out_shape=[
            pltpu.HBM((2 * SEL * BLK, BLK * HEADS), bf16),
            pltpu.HBM((2 * BLK, BLK * HEADS), bf16),
            jax.ShapeDtypeStruct((2 * SEL * BLK, LAT), bf16),
            jax.ShapeDtypeStruct((8 * HALF, 128), bf16),
            jax.ShapeDtypeStruct((8 * HALF, 128), bf16),
        ],
        in_specs=[
            SMEM,
            whole((128, LAT)),
            whole((128, ROPE)),
            whole((8 * HALF, 128)),
            whole((8 * HALF, 128)),
            rows(LAT),
            rows(ROPE),
            rows(LAT),
        ],
        out_specs=[
            pl.BlockSpec((SEL * BLK, TILE), lambda i, t: (i, t)),
            pl.BlockSpec((BLK, TILE), lambda i, t: (i, t)),
            pl.BlockSpec((SEL * BLK, LAT), lambda i, t: (i, 0)),
            whole((8 * HALF, 128)),
            whole((8 * HALF, 128)),
        ],
        scratch_shapes=[
            pltpu.VMEM((2, 576, 128), bf16),
            pltpu.VMEM((SEL * BLK, LAT), bf16),
            pltpu.VMEM((SEL * BLK, ROPE), bf16),
            pltpu.VMEM(((SEL - 1) * BLK, LAT), f32),
            pltpu.VMEM(((SEL - 1) * BLK, ROPE), f32),
        ],
        compiler_params=PARAMS,
        name="attention",
    )(meta, lat, rot, mine, other, q, qr, do)


def output_kernel(probs_ref, ds_ref, keys, q_ref, qr_ref, do_ref, out_ref, dkl_ref, dkr_ref):
    @pl.when(pl.program_id(1) == 0)
    def _():
        dkl_ref[...] = jnp.zeros_like(dkl_ref)
        dkr_ref[...] = jnp.zeros_like(dkr_ref)

    probs = probs_ref[...]
    out_ref[...] = lax.dot_general(
        probs, keys[...], (((0,), (0,)), ((), ())), preferred_element_type=f32
    ).astype(bf16)
    dscores = ds_ref[...]
    dkl_ref[...] += jnp.dot(dscores, q_ref[...], preferred_element_type=f32) + jnp.dot(
        probs[:BLK], do_ref[...], preferred_element_type=f32
    )
    dkr_ref[...] += jnp.dot(dscores, qr_ref[...], preferred_element_type=f32)


def output(probs, ds, keys, q, qr, do):
    tiles = BLK * HEADS // TILE
    rows = lambda width: pl.BlockSpec((TILE, width), lambda i, t: (i * tiles + t, 0))
    return pl.pallas_call(
        output_kernel,
        grid=(2, tiles),
        out_shape=[
            jax.ShapeDtypeStruct(q.shape, bf16),
            jax.ShapeDtypeStruct((2 * BLK, LAT), f32),
            jax.ShapeDtypeStruct((2 * BLK, ROPE), f32),
        ],
        in_specs=[
            pl.BlockSpec((SEL * BLK, TILE), lambda i, t: (i, t)),
            pl.BlockSpec((BLK, TILE), lambda i, t: (i, t)),
            pl.BlockSpec((SEL * BLK, LAT), lambda i, t: (i, 0)),
            rows(LAT),
            rows(ROPE),
            rows(LAT),
        ],
        out_specs=[
            rows(LAT),
            pl.BlockSpec((BLK, LAT), lambda i, t: (i, 0)),
            pl.BlockSpec((BLK, ROPE), lambda i, t: (i, 0)),
        ],
        compiler_params=PARAMS,
        name="output",
    )(probs, ds, keys, q, qr, do)


def slots_kernel(mine, recv, g):
    g[0:1152] = mine[...]
    g[1152:2304] = recv[...]


def plane_kernel(where_, *refs):
    ins, rest, own, acc = refs[:4], refs[4:8], refs[8:12], refs[12]
    acc[...] = jnp.zeros_like(acc)
    for k in range(4):
        for s in range(16):
            f = where_[k * 16 + s]
            acc[f] = acc[f] + ins[k][s * HALF : (s + 1) * HALF].astype(f32)
    for k in range(4):
        for j in range(16):
            out, row = (own[k], j) if j < 4 else (rest[k], j - 4)
            out[row * HALF : (row + 1) * HALF] = acc[ORDER[k] * 16 + j].astype(out.dtype)


def sum_rows(ins, at):
    total = ins[0][at : at + HALF].astype(f32)
    for part in ins[1:]:
        total = total + part[at : at + HALF].astype(f32)
    return total


def column_kernel(*refs):
    ins, outs = refs[:4], refs[4:7]
    for j in range(12):
        out, row = outs[ORDER.index(j // 4 + 1) - 1], (j % 4) * HALF
        out[row : row + HALF] = sum_rows(ins, j * HALF).astype(bf16)


def owner_kernel(*refs):
    ins, outs = refs[:7], refs[7:9]
    for j in range(4):
        row = (j % 2) * HALF
        outs[j // 2][row : row + HALF] = sum_rows(ins, j * HALF)


def half_sum_kernel(meta, mine, recv, dkl, dkr, out, units):
    c = meta[0]
    units[c] = mine[...]
    units[1 - c] = recv[...]
    for i in range(2):
        lo, hi = slice(i * 64, i * 64 + 32), slice(i * 64 + 32, i * 64 + 64)
        packed = jnp.concatenate([dkr[lo, :], dkr[hi, :]], axis=1)
        for n in range(18):
            if n < 16:
                l, r = n // 4, n % 4
                own = dkl[i * 64 + r * UNIT : i * 64 + (r + 1) * UNIT, l * 128 : (l + 1) * 128]
            else:
                own = packed[(n - 16) * UNIT : (n - 15) * UNIT]
            row = i * HALF + (n % 9) * UNIT
            to = (i * 18 + n) * UNIT
            out[to : to + UNIT] = (units[n // 9, row : row + UNIT, :] + own).astype(bf16)


def final_kernel(mine, recv, cosine, sine, lat_out, rope_out):
    parts = []
    for i in range(2):
        for n in range(16):
            l, r = n // 4, n % 4
            at = (i * 18 + n) * UNIT
            lat_out[i * 64 + r * UNIT : i * 64 + (r + 1) * UNIT, l * 128 : (l + 1) * 128] = mine[
                at : at + UNIT
            ].astype(f32) + recv[at : at + UNIT].astype(f32)
        at = (i * 18 + 16) * UNIT
        packed = mine[at : at + 32].astype(f32) + recv[at : at + 32].astype(f32)
        parts += [packed[:, :64], packed[:, 64:]]
    g = jnp.concatenate(parts, axis=0).T
    lo, hi, cs, sn = g[:32], g[32:], cosine[...], sine[...]
    rope_out[...] = jnp.concatenate([lo * cs + hi * sn, hi * cs - lo * sn], axis=0)


def shards(latent, rope_key, queries, query_rope, grad_out, sel_blocks):
    x, y, z, c = [lax.axis_index(a) for a in "xyzc"]
    ctx = ((x * 4 + y) * 4 + z) * 2 + c
    meta = jnp.stack([c, ctx * 2]).astype(jnp.int32)

    positions = ctx * 128 + jnp.arange(128, dtype=jnp.int32)
    freq_steps = jnp.arange(ROPE // 2, dtype=f32)
    inverse_freq = rope_base ** (-2.0 * freq_steps / ROPE)
    angles = positions.astype(f32)[None, :] * inverse_freq[:, None]
    cosine, sine = jnp.cos(angles), jnp.sin(angles)

    sel_row = sel_blocks[:, 1:].reshape(1, 8).astype(bf16)
    sel_unit = jnp.broadcast_to(jnp.pad(sel_row, ((0, 0), (0, 120))), (UNIT, 128))
    mine, other, rot = call(
        prep_kernel,
        (meta, latent, rope_key.T, cosine, sine, sel_unit),
        [((304, 128), bf16), ((304, 128), bf16), ((128, ROPE), bf16)],
        [pltpu.VMEM((2, 304, 128), bf16)],
        scalars=1,
        name="prep",
    )
    chip, sel = call(
        chip_kernel, (mine, swap(other, "c")), [((576, 128), bf16), ((UNIT, 128), bf16)], name="chip"
    )

    def all_of(a, phase):
        return [a] + [exchange(a, phase, k) for k in (1, 2, 3)]

    def each_of(parts, phase):
        return [exchange(part, phase, k) for part, k in zip(parts, ORDER[1:])]

    own_plane = all_of(chip, "v")
    lines = all_of(chip, "u")
    got = lax.optimization_barrier((*own_plane[1:], *lines[1:]))
    own_plane = [chip, *got[:3]]
    (line,) = call(line_kernel, got[3:], [((1728, 128), bf16)], name="line")
    rest_plane = all_of(line, "v")

    asked = jnp.stack([t[:2, :8] for t in all_of(sel, "w")]).astype(jnp.int32).reshape(4, 16)
    sx, sy, sz = asked >> 6, (asked >> 4) & 3, (asked >> 2) & 3
    local = jnp.where(((asked >> 1) & 1) == c, 0, 2) + (asked & 1)
    on_v = jnp.where(c == 0, x ^ sx, y ^ sy)
    on_w = jnp.where(c == 0, y ^ sy, x ^ sx)
    pos = on_v * 16 + (z ^ sz) * 4 + local
    pack_at = pos.reshape(-1)
    add_at = jnp.where(on_w == 0, pos, 64).reshape(-1)
    merge_at = on_w[0]

    packed = call(
        pack_kernel,
        [pack_at] + own_plane + rest_plane,
        [((2304, 128), bf16)] * 4,
        [pltpu.VMEM((64, HALF, 128), bf16)],
        scalars=1,
        name="pack",
    )
    got = [packed[0]] + each_of(packed[1:], "w")
    key_mine, key_other = call(
        merge_kernel,
        [merge_at] + got,
        [((8 * HALF, 128), bf16)] * 2,
        [pltpu.VMEM((64, HALF, 128), bf16)],
        scalars=1,
        name="merge",
    )
    key_recv = swap(key_other, "c")

    q = queries.reshape(128 * HEADS, LAT)
    do = grad_out.reshape(128 * HEADS, LAT)
    qr = query_rope.reshape(128 * HEADS, ROPE)
    probs, ds, keys, g_mine, g_other = attention(meta, latent, rot, key_mine, key_recv, q, qr, do)

    (slots,) = call(slots_kernel, (g_mine, swap(g_other, "c")), [((2304, 128), bf16)], name="slots")
    keys, slots = lax.optimization_barrier((keys, slots))
    out, dkl, dkr = output(probs, ds, keys, q, qr, do)
    add_at, dkl, dkr = lax.optimization_barrier((add_at, dkl, dkr))
    sums = call(
        plane_kernel,
        [add_at] + all_of(slots, "w"),
        [((rows, 128), bf16 if k else f32) for rows in (1728, 576) for k in range(4)],
        [pltpu.VMEM((65, HALF, 128), f32)],
        scalars=1,
        name="plane",
    )
    rest, own = sums[:4], sums[4:]
    columns = call(
        column_kernel, [rest[0]] + each_of(rest[1:], "v"), [((576, 128), bf16)] * 3, name="column"
    )
    got = [own[0]] + each_of(own[1:], "v") + each_of(columns, "u")
    f_mine, f_other = call(owner_kernel, got, [((288, 128), f32)] * 2, name="owner")
    (total,) = call(
        half_sum_kernel,
        (meta, f_mine, swap(f_other, "c"), dkl, dkr),
        [((576, 128), bf16)],
        [pltpu.VMEM((2, 288, 128), f32)],
        scalars=1,
        name="half_sum",
    )
    d_latent, d_rope_key = call(
        final_kernel,
        (total, swap(total, "h"), cosine, sine),
        [((128, LAT), f32), ((ROPE, 128), f32)],
        name="final",
    )
    return out.reshape(128, HEADS, LAT), d_latent, d_rope_key.T


def solution(mesh):
    lines = Mesh(mesh.devices.reshape(4, 4, 4, 2, 2), MESH)
    ctx = ("x", "y", "z", "c")
    return jax.shard_map(
        shards,
        mesh=lines,
        in_specs=(
            P(ctx, None),
            P(ctx, None),
            P(ctx, "h", None),
            P(ctx, "h"),
            P(ctx, "h", None),
            P(ctx, None),
        ),
        out_specs=(P(ctx, "h", None), P(ctx, None), P(ctx, None)),
        check_vma=False,
    )
```

```python
import functools

import jax
import jax.numpy as jnp
from jax import lax
from jax.experimental import pallas as pl
from jax.experimental.pallas import tpu as pltpu
from jax.sharding import Mesh, PartitionSpec as P

BLK = 64
SEL = 5
LAT = 512
ROPE = 64
HEADS = 32
UNIT = 16
HALF = 144
TILE = 1024
ORDER = (0, 3, 2, 1)

softmax_scale = 192.0 ** (-0.5)
rope_base = 10000.0
log2_e = 1.4426950408889634

bf16 = jnp.bfloat16
f32 = jnp.float32
VMEM = pl.BlockSpec(memory_space=pltpu.VMEM)
SMEM = pl.BlockSpec(memory_space=pltpu.SMEM)
PARAMS = pltpu.CompilerParams(vmem_limit_bytes=48 * 1024 * 1024)


def call(kernel, ins, outs, scratch=(), scalars=0, name=None):
    specs = [SMEM] * scalars + [VMEM] * (len(ins) - scalars)
    return pl.pallas_call(
        kernel,
        out_shape=[jax.ShapeDtypeStruct(s, d) for s, d in outs],
        in_specs=specs,
        out_specs=[VMEM] * len(outs),
        scratch_shapes=list(scratch),
        compiler_params=PARAMS,
        name=name,
    )(*ins)


MESH = ("x", "y", "z", "c", "h")


def partner(place, phase, k):
    x, y, z, c, h = place
    axis = "z" if phase == "u" else "xy"[c if phase == "v" else 1 - c]
    if axis == "x":
        x ^= k
    elif axis == "y":
        y ^= k
    else:
        ring = h * 4 + z
        if k == 3:
            ring = (ring + (1 if ring % 2 else 7)) % 8
        else:
            ring ^= k
        h, z = ring // 4, ring % 4
    return x, y, z, c, h


def number(place):
    x, y, z, c, h = place
    return (((x * 4 + y) * 4 + z) * 2 + c) * 2 + h


def exchange(a, phase, k):
    places = [(i // 64, i // 16 % 4, i // 4 % 4, i // 2 % 2, i % 2) for i in range(256)]
    return lax.ppermute(a, MESH, [(number(p), number(partner(p, phase, k))) for p in places])


def swap(a, axis):
    return lax.ppermute(a, axis, [(0, 1), (1, 0)])


def prep_kernel(meta, lat, rope, cosine, sine, sel, mine, other, rot_out, units):
    c = meta[0]
    x = rope[...].astype(f32)
    lo, hi = x[:32], x[32:]
    rot = jnp.concatenate(
        [lo * cosine[...] - hi * sine[...], hi * cosine[...] + lo * sine[...]], axis=0
    ).T.astype(bf16)
    rot_out[...] = rot
    for i in range(2):
        packed = jnp.concatenate([rot[i * 64 : i * 64 + 32], rot[i * 64 + 32 : i * 64 + 64]], axis=1)
        for n in range(18):
            if n < 16:
                l, r = n // 4, n % 4
                v = lat[i * 64 + r * UNIT : i * 64 + (r + 1) * UNIT, l * 128 : (l + 1) * 128]
            else:
                v = packed[(n - 16) * UNIT : (n - 15) * UNIT]
            row = i * HALF + (n % 9) * UNIT
            units[n // 9, row : row + UNIT, :] = v
    for half in range(2):
        units[half, 288:304, :] = sel[...]
    mine[...] = units[c]
    other[...] = units[1 - c]


def chip_kernel(mine, recv, x, sel):
    x[0:288] = mine[0:288]
    x[288:576] = recv[0:288]
    row = lax.broadcasted_iota(jnp.int32, (UNIT, 128), 0)
    sel[...] = jnp.where(
        row == 0, mine[288:304].astype(f32), recv[288:304].astype(f32)
    ).astype(bf16)


def line_kernel(*refs):
    for k in range(3):
        refs[3][k * 576 : (k + 1) * 576] = refs[k][...]


def pack_kernel(where_, *refs):
    own, rest, outs, held = refs[:4], refs[4:8], refs[8:12], refs[12]
    for k in range(4):
        held[k * 16 : k * 16 + 4] = own[k][...].reshape(4, HALF, 128)
        held[k * 16 + 4 : k * 16 + 16] = rest[k][...].reshape(12, HALF, 128)
    for k in range(4):
        for s in range(16):
            outs[k][s * HALF : (s + 1) * HALF] = held[where_[ORDER[k] * 16 + s]]


def merge_kernel(where_, *refs):
    ins, mine, other, held = refs[:4], refs[4], refs[5], refs[6]
    for k in range(4):
        held[ORDER[k] * 16 : (ORDER[k] + 1) * 16] = ins[k][...].reshape(16, HALF, 128)
    for s in range(16):
        out = mine if s < 8 else other
        row = (s % 8) * HALF
        out[row : row + HALF] = held[where_[s] * 16 + s]


def attention_kernel(
    meta, lat, rot, mine, other, q_ref, qr_ref, do_ref,
    probs_ref, ds_ref, keys_out, gm_ref, go_ref,
    units, keys, keys_r, acc, acc_r,
):
    i, t = pl.program_id(0), pl.program_id(1)
    c = meta[0]
    block = meta[1] + i

    @pl.when(t == 0)
    def _():
        rows = pl.ds(pl.multiple_of(i * BLK, BLK), BLK)
        keys[0:BLK] = lat[rows, :]
        keys_r[0:BLK] = rot[rows, :]
        part = pl.ds(pl.multiple_of(i * 576, 576), 576)
        units[c] = mine[part, :]
        units[1 - c] = other[part, :]
        for s in range(4):
            base = (s + 1) * BLK
            for n in range(16):
                row = s * HALF + (n % 9) * UNIT
                l, r = n // 4, n % 4
                keys[base + r * UNIT : base + (r + 1) * UNIT, l * 128 : (l + 1) * 128] = units[
                    n // 9, row : row + UNIT, :
                ]
            packed = units[1, s * HALF + 112 : s * HALF + 144, :]
            keys_r[base : base + 32] = packed[:, :64]
            keys_r[base + 32 : base + 64] = packed[:, 64:]
        keys_out[...] = keys[...]
        acc[...] = jnp.zeros_like(acc)
        acc_r[...] = jnp.zeros_like(acc_r)

    nt = (((1,), (1,)), ((), ()))
    limit = jnp.minimum(block + 1, SEL) * BLK
    part = TILE // 4
    grad = jnp.zeros(((SEL - 1) * BLK, LAT), f32)
    grad_r = jnp.zeros(((SEL - 1) * BLK, ROPE), f32)
    raws, dps = [], []
    for j in range(4):
        rows = slice(j * part, (j + 1) * part)
        q, qr, do = q_ref[rows, :], qr_ref[rows, :], do_ref[rows, :]
        raw = lax.dot_general(keys[...], q, nt, preferred_element_type=f32)
        raw = raw + lax.dot_general(keys_r[...], qr, nt, preferred_element_type=f32)
        raws.append(raw)
        dps.append(lax.dot_general(keys[...], do, nt, preferred_element_type=f32))
    for j in range(4):
        rows = slice(j * part, (j + 1) * part)
        q, qr, do = q_ref[rows, :], qr_ref[rows, :], do_ref[rows, :]
        raw, dprobs = raws[j], dps[j]
        key_row = lax.broadcasted_iota(jnp.int32, (BLK, part), 0)
        query = lax.broadcasted_iota(jnp.int32, (BLK, part), 1) // HEADS + t * (TILE // HEADS) + j * (part // HEADS)
        bands = [jnp.where(key_row <= query, raw[:BLK], -jnp.inf)]
        for s in range(1, SEL):
            bands.append(raw[s * BLK : (s + 1) * BLK] + jnp.where(s * BLK < limit, 0.0, -jnp.inf))
        raw = jnp.concatenate(bands, axis=0)
        top = jnp.max(raw, axis=0, keepdims=True)
        expon = jnp.exp2((raw - top) * (softmax_scale * log2_e))
        probs = expon * (1.0 / jnp.sum(expon, axis=0, keepdims=True))
        probs_low = probs.astype(bf16)
        row_delta = jnp.sum(probs * dprobs, axis=0, keepdims=True)
        dscores = (probs * ((dprobs - row_delta) * softmax_scale)).astype(bf16)
        probs_ref[:, rows] = probs_low
        ds_ref[:, rows] = dscores[:BLK]
        grad = grad + jnp.dot(dscores[BLK:], q, preferred_element_type=f32)
        grad = grad + jnp.dot(probs_low[BLK:], do, preferred_element_type=f32)
        grad_r = grad_r + jnp.dot(dscores[BLK:], qr, preferred_element_type=f32)
    acc[...] += grad
    acc_r[...] += grad_r

    @pl.when(t == pl.num_programs(1) - 1)
    def _():
        for s in range(4):
            base = s * BLK
            packed = jnp.concatenate(
                [acc_r[base : base + 32, :], acc_r[base + 32 : base + 64, :]], axis=1
            )
            for n in range(18):
                m = n % 9
                if n < 16:
                    l, r = n // 4, n % 4
                    v = acc[base + r * UNIT : base + (r + 1) * UNIT, l * 128 : (l + 1) * 128]
                else:
                    v = packed[(n - 16) * UNIT : (n - 15) * UNIT]
                row = s * HALF + m * UNIT
                units[n // 9, row : row + UNIT, :] = v.astype(bf16)
        part = pl.ds(pl.multiple_of(i * 576, 576), 576)
        gm_ref[part, :] = units[c]
        go_ref[part, :] = units[1 - c]


def attention(meta, lat, rot, mine, other, q, qr, do):
    tiles = BLK * HEADS // TILE
    whole = lambda shape: pl.BlockSpec(shape, lambda i, t: (0, 0))
    rows = lambda width: pl.BlockSpec((TILE, width), lambda i, t: (i * tiles + t, 0))
    return pl.pallas_call(
        attention_kernel,
        grid=(2, tiles),
        out_shape=[
            pltpu.HBM((2 * SEL * BLK, BLK * HEADS), bf16),
            pltpu.HBM((2 * BLK, BLK * HEADS), bf16),
            jax.ShapeDtypeStruct((2 * SEL * BLK, LAT), bf16),
            jax.ShapeDtypeStruct((8 * HALF, 128), bf16),
            jax.ShapeDtypeStruct((8 * HALF, 128), bf16),
        ],
        in_specs=[
            SMEM,
            whole((128, LAT)),
            whole((128, ROPE)),
            whole((8 * HALF, 128)),
            whole((8 * HALF, 128)),
            rows(LAT),
            rows(ROPE),
            rows(LAT),
        ],
        out_specs=[
            pl.BlockSpec((SEL * BLK, TILE), lambda i, t: (i, t)),
            pl.BlockSpec((BLK, TILE), lambda i, t: (i, t)),
            pl.BlockSpec((SEL * BLK, LAT), lambda i, t: (i, 0)),
            whole((8 * HALF, 128)),
            whole((8 * HALF, 128)),
        ],
        scratch_shapes=[
            pltpu.VMEM((2, 576, 128), bf16),
            pltpu.VMEM((SEL * BLK, LAT), bf16),
            pltpu.VMEM((SEL * BLK, ROPE), bf16),
            pltpu.VMEM(((SEL - 1) * BLK, LAT), f32),
            pltpu.VMEM(((SEL - 1) * BLK, ROPE), f32),
        ],
        compiler_params=PARAMS,
        name="attention",
    )(meta, lat, rot, mine, other, q, qr, do)


def output_kernel(probs_ref, ds_ref, keys, q_ref, qr_ref, do_ref, out_ref, dkl_ref, dkr_ref):
    @pl.when(pl.program_id(1) == 0)
    def _():
        dkl_ref[...] = jnp.zeros_like(dkl_ref)
        dkr_ref[...] = jnp.zeros_like(dkr_ref)

    probs = probs_ref[...]
    out_ref[...] = lax.dot_general(
        probs, keys[...], (((0,), (0,)), ((), ())), preferred_element_type=f32
    ).astype(bf16)
    dscores = ds_ref[...]
    dkl_ref[...] += jnp.dot(dscores, q_ref[...], preferred_element_type=f32) + jnp.dot(
        probs[:BLK], do_ref[...], preferred_element_type=f32
    )
    dkr_ref[...] += jnp.dot(dscores, qr_ref[...], preferred_element_type=f32)


def output(probs, ds, keys, q, qr, do):
    tiles = BLK * HEADS // TILE
    rows = lambda width: pl.BlockSpec((TILE, width), lambda i, t: (i * tiles + t, 0))
    return pl.pallas_call(
        output_kernel,
        grid=(2, tiles),
        out_shape=[
            jax.ShapeDtypeStruct(q.shape, bf16),
            jax.ShapeDtypeStruct((2 * BLK, LAT), f32),
            jax.ShapeDtypeStruct((2 * BLK, ROPE), f32),
        ],
        in_specs=[
            pl.BlockSpec((SEL * BLK, TILE), lambda i, t: (i, t)),
            pl.BlockSpec((BLK, TILE), lambda i, t: (i, t)),
            pl.BlockSpec((SEL * BLK, LAT), lambda i, t: (i, 0)),
            rows(LAT),
            rows(ROPE),
            rows(LAT),
        ],
        out_specs=[
            rows(LAT),
            pl.BlockSpec((BLK, LAT), lambda i, t: (i, 0)),
            pl.BlockSpec((BLK, ROPE), lambda i, t: (i, 0)),
        ],
        compiler_params=PARAMS,
        name="output",
    )(probs, ds, keys, q, qr, do)


def slots_kernel(mine, recv, g):
    g[0:1152] = mine[...]
    g[1152:2304] = recv[...]


def plane_kernel(where_, *refs):
    ins, rest, own, acc = refs[:4], refs[4:8], refs[8:12], refs[12]
    acc[...] = jnp.zeros_like(acc)
    for k in range(4):
        for s in range(16):
            f = where_[k * 16 + s]
            acc[f] = acc[f] + ins[k][s * HALF : (s + 1) * HALF].astype(f32)
    for k in range(4):
        for j in range(16):
            out, row = (own[k], j) if j < 4 else (rest[k], j - 4)
            out[row * HALF : (row + 1) * HALF] = acc[ORDER[k] * 16 + j].astype(out.dtype)


def sum_rows(ins, at):
    total = ins[0][at : at + HALF].astype(f32)
    for part in ins[1:]:
        total = total + part[at : at + HALF].astype(f32)
    return total


def column_kernel(*refs):
    ins, outs = refs[:4], refs[4:7]
    for j in range(12):
        out, row = outs[ORDER.index(j // 4 + 1) - 1], (j % 4) * HALF
        out[row : row + HALF] = sum_rows(ins, j * HALF).astype(bf16)


def owner_kernel(*refs):
    ins, outs = refs[:7], refs[7:9]
    for j in range(4):
        row = (j % 2) * HALF
        outs[j // 2][row : row + HALF] = sum_rows(ins, j * HALF)


def half_sum_kernel(meta, mine, recv, dkl, dkr, out, units):
    c = meta[0]
    units[c] = mine[...]
    units[1 - c] = recv[...]
    for i in range(2):
        lo, hi = slice(i * 64, i * 64 + 32), slice(i * 64 + 32, i * 64 + 64)
        packed = jnp.concatenate([dkr[lo, :], dkr[hi, :]], axis=1)
        for n in range(18):
            if n < 16:
                l, r = n // 4, n % 4
                own = dkl[i * 64 + r * UNIT : i * 64 + (r + 1) * UNIT, l * 128 : (l + 1) * 128]
            else:
                own = packed[(n - 16) * UNIT : (n - 15) * UNIT]
            row = i * HALF + (n % 9) * UNIT
            to = (i * 18 + n) * UNIT
            out[to : to + UNIT] = (units[n // 9, row : row + UNIT, :] + own).astype(bf16)


def final_kernel(mine, recv, cosine, sine, lat_out, rope_out):
    parts = []
    for i in range(2):
        for n in range(16):
            l, r = n // 4, n % 4
            at = (i * 18 + n) * UNIT
            lat_out[i * 64 + r * UNIT : i * 64 + (r + 1) * UNIT, l * 128 : (l + 1) * 128] = mine[
                at : at + UNIT
            ].astype(f32) + recv[at : at + UNIT].astype(f32)
        at = (i * 18 + 16) * UNIT
        packed = mine[at : at + 32].astype(f32) + recv[at : at + 32].astype(f32)
        parts += [packed[:, :64], packed[:, 64:]]
    g = jnp.concatenate(parts, axis=0).T
    lo, hi, cs, sn = g[:32], g[32:], cosine[...], sine[...]
    rope_out[...] = jnp.concatenate([lo * cs + hi * sn, hi * cs - lo * sn], axis=0)


def shards(latent, rope_key, queries, query_rope, grad_out, sel_blocks):
    x, y, z, c = [lax.axis_index(a) for a in "xyzc"]
    ctx = ((x * 4 + y) * 4 + z) * 2 + c
    meta = jnp.stack([c, ctx * 2]).astype(jnp.int32)

    positions = ctx * 128 + jnp.arange(128, dtype=jnp.int32)
    freq_steps = jnp.arange(ROPE // 2, dtype=f32)
    inverse_freq = rope_base ** (-2.0 * freq_steps / ROPE)
    angles = positions.astype(f32)[None, :] * inverse_freq[:, None]
    cosine, sine = jnp.cos(angles), jnp.sin(angles)

    sel_row = sel_blocks[:, 1:].reshape(1, 8).astype(bf16)
    sel_unit = jnp.broadcast_to(jnp.pad(sel_row, ((0, 0), (0, 120))), (UNIT, 128))
    mine, other, rot = call(
        prep_kernel,
        (meta, latent, rope_key.T, cosine, sine, sel_unit),
        [((304, 128), bf16), ((304, 128), bf16), ((128, ROPE), bf16)],
        [pltpu.VMEM((2, 304, 128), bf16)],
        scalars=1,
        name="prep",
    )
    chip, sel = call(
        chip_kernel, (mine, swap(other, "c")), [((576, 128), bf16), ((UNIT, 128), bf16)], name="chip"
    )

    def all_of(a, phase):
        return [a] + [exchange(a, phase, k) for k in (1, 2, 3)]

    def each_of(parts, phase):
        return [exchange(part, phase, k) for part, k in zip(parts, ORDER[1:])]

    own_plane = all_of(chip, "v")
    lines = all_of(chip, "u")
    got = lax.optimization_barrier((*own_plane[1:], *lines[1:]))
    own_plane = [chip, *got[:3]]
    (line,) = call(line_kernel, got[3:], [((1728, 128), bf16)], name="line")
    rest_plane = all_of(line, "v")

    asked = jnp.stack([t[:2, :8] for t in all_of(sel, "w")]).astype(jnp.int32).reshape(4, 16)
    sx, sy, sz = asked >> 6, (asked >> 4) & 3, (asked >> 2) & 3
    local = jnp.where(((asked >> 1) & 1) == c, 0, 2) + (asked & 1)
    on_v = jnp.where(c == 0, x ^ sx, y ^ sy)
    on_w = jnp.where(c == 0, y ^ sy, x ^ sx)
    pos = on_v * 16 + (z ^ sz) * 4 + local
    pack_at = pos.reshape(-1)
    add_at = jnp.where(on_w == 0, pos, 64).reshape(-1)
    merge_at = on_w[0]

    packed = call(
        pack_kernel,
        [pack_at] + own_plane + rest_plane,
        [((2304, 128), bf16)] * 4,
        [pltpu.VMEM((64, HALF, 128), bf16)],
        scalars=1,
        name="pack",
    )
    got = [packed[0]] + each_of(packed[1:], "w")
    merge_at, qr = lax.optimization_barrier((merge_at, query_rope.reshape(128 * HEADS, ROPE)))
    key_mine, key_other = call(
        merge_kernel,
        [merge_at] + got,
        [((8 * HALF, 128), bf16)] * 2,
        [pltpu.VMEM((64, HALF, 128), bf16)],
        scalars=1,
        name="merge",
    )
    key_recv = swap(key_other, "c")

    q = queries.reshape(128 * HEADS, LAT)
    do = grad_out.reshape(128 * HEADS, LAT)
    probs, ds, keys, g_mine, g_other = attention(meta, latent, rot, key_mine, key_recv, q, qr, do)

    (slots,) = call(slots_kernel, (g_mine, swap(g_other, "c")), [((2304, 128), bf16)], name="slots")
    keys, slots = lax.optimization_barrier((keys, slots))
    out, dkl, dkr = output(probs, ds, keys, q, qr, do)
    add_at, dkl, dkr = lax.optimization_barrier((add_at, dkl, dkr))
    sums = call(
        plane_kernel,
        [add_at] + all_of(slots, "w"),
        [((rows, 128), bf16 if k else f32) for rows in (1728, 576) for k in range(4)],
        [pltpu.VMEM((65, HALF, 128), f32)],
        scalars=1,
        name="plane",
    )
    rest, own = sums[:4], sums[4:]
    columns = call(
        column_kernel, [rest[0]] + each_of(rest[1:], "v"), [((576, 128), bf16)] * 3, name="column"
    )
    got = [own[0]] + each_of(own[1:], "v") + each_of(columns, "u")
    f_mine, f_other = call(owner_kernel, got, [((288, 128), f32)] * 2, name="owner")
    (total,) = call(
        half_sum_kernel,
        (meta, f_mine, swap(f_other, "c"), dkl, dkr),
        [((576, 128), bf16)],
        [pltpu.VMEM((2, 288, 128), f32)],
        scalars=1,
        name="half_sum",
    )
    d_latent, d_rope_key = call(
        final_kernel,
        (total, swap(total, "h"), cosine, sine),
        [((128, LAT), f32), ((ROPE, 128), f32)],
        name="final",
    )
    return out.reshape(128, HEADS, LAT), d_latent, d_rope_key.T


def solution(mesh):
    lines = Mesh(mesh.devices.reshape(4, 4, 4, 2, 2), MESH)
    ctx = ("x", "y", "z", "c")
    return jax.shard_map(
        shards,
        mesh=lines,
        in_specs=(
            P(ctx, None),
            P(ctx, None),
            P(ctx, "h", None),
            P(ctx, "h"),
            P(ctx, "h", None),
            P(ctx, None),
        ),
        out_specs=(P(ctx, "h", None), P(ctx, None), P(ctx, None)),
        check_vma=False,
    )
```

```python
import functools

import jax
import jax.numpy as jnp
from jax import lax
from jax.experimental import pallas as pl
from jax.experimental.pallas import tpu as pltpu
from jax.sharding import Mesh, PartitionSpec as P

BLK = 64
SEL = 5
LAT = 512
ROPE = 64
HEADS = 32
UNIT = 16
HALF = 144
TILE = 1024
ORDER = (0, 3, 2, 1)

softmax_scale = 192.0 ** (-0.5)
rope_base = 10000.0
log2_e = 1.4426950408889634

bf16 = jnp.bfloat16
f32 = jnp.float32
VMEM = pl.BlockSpec(memory_space=pltpu.VMEM)
SMEM = pl.BlockSpec(memory_space=pltpu.SMEM)
PARAMS = pltpu.CompilerParams(vmem_limit_bytes=44 * 1024 * 1024)


def call(kernel, ins, outs, scratch=(), scalars=0, name=None):
    specs = [SMEM] * scalars + [VMEM] * (len(ins) - scalars)
    return pl.pallas_call(
        kernel,
        out_shape=[jax.ShapeDtypeStruct(s, d) for s, d in outs],
        in_specs=specs,
        out_specs=[VMEM] * len(outs),
        scratch_shapes=list(scratch),
        compiler_params=PARAMS,
        name=name,
    )(*ins)


MESH = ("x", "y", "z", "c", "h")


def partner(place, phase, k):
    x, y, z, c, h = place
    axis = "z" if phase == "u" else "xy"[c if phase == "v" else 1 - c]
    if axis == "x":
        x ^= k
    elif axis == "y":
        y ^= k
    else:
        ring = h * 4 + z
        if k == 3:
            ring = (ring + (1 if ring % 2 else 7)) % 8
        else:
            ring ^= k
        h, z = ring // 4, ring % 4
    return x, y, z, c, h


def number(place):
    x, y, z, c, h = place
    return (((x * 4 + y) * 4 + z) * 2 + c) * 2 + h


def exchange(a, phase, k):
    places = [(i // 64, i // 16 % 4, i // 4 % 4, i // 2 % 2, i % 2) for i in range(256)]
    return lax.ppermute(a, MESH, [(number(p), number(partner(p, phase, k))) for p in places])


def swap(a, axis):
    return lax.ppermute(a, axis, [(0, 1), (1, 0)])


def prep_kernel(meta, lat, rope, cosine, sine, sel, mine, other, rot_out, units):
    c = meta[0]
    x = rope[...].astype(f32)
    lo, hi = x[:32], x[32:]
    rot = jnp.concatenate(
        [lo * cosine[...] - hi * sine[...], hi * cosine[...] + lo * sine[...]], axis=0
    ).T.astype(bf16)
    rot_out[...] = rot
    for i in range(2):
        packed = jnp.concatenate([rot[i * 64 : i * 64 + 32], rot[i * 64 + 32 : i * 64 + 64]], axis=1)
        for n in range(18):
            if n < 16:
                l, r = n // 4, n % 4
                v = lat[i * 64 + r * UNIT : i * 64 + (r + 1) * UNIT, l * 128 : (l + 1) * 128]
            else:
                v = packed[(n - 16) * UNIT : (n - 15) * UNIT]
            row = i * HALF + (n % 9) * UNIT
            units[n // 9, row : row + UNIT, :] = v
    for half in range(2):
        units[half, 288:304, :] = sel[...]
    mine[...] = units[c]
    other[...] = units[1 - c]


def chip_kernel(mine, recv, x, sel):
    x[0:288] = mine[0:288]
    x[288:576] = recv[0:288]
    row = lax.broadcasted_iota(jnp.int32, (UNIT, 128), 0)
    sel[...] = jnp.where(
        row == 0, mine[288:304].astype(f32), recv[288:304].astype(f32)
    ).astype(bf16)


def line_kernel(*refs):
    for k in range(3):
        refs[3][k * 576 : (k + 1) * 576] = refs[k][...]


def pack_kernel(where_, *refs):
    own, rest, outs, held = refs[:4], refs[4:8], refs[8:12], refs[12]
    for k in range(4):
        held[k * 16 : k * 16 + 4] = own[k][...].reshape(4, HALF, 128)
        held[k * 16 + 4 : k * 16 + 16] = rest[k][...].reshape(12, HALF, 128)
    for k in range(4):
        for s in range(16):
            outs[k][s * HALF : (s + 1) * HALF] = held[where_[ORDER[k] * 16 + s]]


def merge_kernel(where_, *refs):
    ins, mine, other, held = refs[:4], refs[4], refs[5], refs[6]
    for k in range(4):
        held[ORDER[k] * 16 : (ORDER[k] + 1) * 16] = ins[k][...].reshape(16, HALF, 128)
    for s in range(16):
        out = mine if s < 8 else other
        row = (s % 8) * HALF
        out[row : row + HALF] = held[where_[s] * 16 + s]


def attention_kernel(
    meta, lat, rot, mine, other, q_ref, qr_ref, do_ref,
    probs_ref, ds_ref, keys_out, gm_ref, go_ref,
    units, keys, keys_r, acc, acc_r,
):
    i, t = pl.program_id(0), pl.program_id(1)
    c = meta[0]
    block = meta[1] + i

    @pl.when(t == 0)
    def _():
        rows = pl.ds(pl.multiple_of(i * BLK, BLK), BLK)
        keys[0:BLK] = lat[rows, :]
        keys_r[0:BLK] = rot[rows, :]
        part = pl.ds(pl.multiple_of(i * 576, 576), 576)
        units[c] = mine[part, :]
        units[1 - c] = other[part, :]
        for s in range(4):
            base = (s + 1) * BLK
            for n in range(16):
                row = s * HALF + (n % 9) * UNIT
                l, r = n // 4, n % 4
                keys[base + r * UNIT : base + (r + 1) * UNIT, l * 128 : (l + 1) * 128] = units[
                    n // 9, row : row + UNIT, :
                ]
            packed = units[1, s * HALF + 112 : s * HALF + 144, :]
            keys_r[base : base + 32] = packed[:, :64]
            keys_r[base + 32 : base + 64] = packed[:, 64:]
        keys_out[...] = keys[...]
        acc[...] = jnp.zeros_like(acc)
        acc_r[...] = jnp.zeros_like(acc_r)

    nt = (((1,), (1,)), ((), ()))
    limit = jnp.minimum(block + 1, SEL) * BLK
    part = TILE // 4
    grad = jnp.zeros(((SEL - 1) * BLK, LAT), f32)
    grad_r = jnp.zeros(((SEL - 1) * BLK, ROPE), f32)
    raws, dps = [], []
    for j in range(4):
        rows = slice(j * part, (j + 1) * part)
        q, qr, do = q_ref[rows, :], qr_ref[rows, :], do_ref[rows, :]
        raw = lax.dot_general(keys[...], q, nt, preferred_element_type=f32)
        raw = raw + lax.dot_general(keys_r[...], qr, nt, preferred_element_type=f32)
        raws.append(raw)
        dps.append(lax.dot_general(keys[...], do, nt, preferred_element_type=f32))
    for j in range(4):
        rows = slice(j * part, (j + 1) * part)
        q, qr, do = q_ref[rows, :], qr_ref[rows, :], do_ref[rows, :]
        raw, dprobs = raws[j], dps[j]
        key_row = lax.broadcasted_iota(jnp.int32, (BLK, part), 0)
        query = lax.broadcasted_iota(jnp.int32, (BLK, part), 1) // HEADS + t * (TILE // HEADS) + j * (part // HEADS)
        bands = [jnp.where(key_row <= query, raw[:BLK], -jnp.inf)]
        for s in range(1, SEL):
            bands.append(raw[s * BLK : (s + 1) * BLK] + jnp.where(s * BLK < limit, 0.0, -jnp.inf))
        raw = jnp.concatenate(bands, axis=0)
        top = jnp.max(raw, axis=0, keepdims=True)
        expon = jnp.exp2((raw - top) * (softmax_scale * log2_e))
        probs = expon * (1.0 / jnp.sum(expon, axis=0, keepdims=True))
        probs_low = probs.astype(bf16)
        row_delta = jnp.sum(probs * dprobs, axis=0, keepdims=True)
        dscores = (probs * ((dprobs - row_delta) * softmax_scale)).astype(bf16)
        probs_ref[:, rows] = probs_low
        ds_ref[:, rows] = dscores[:BLK]
        grad = grad + jnp.dot(dscores[BLK:], q, preferred_element_type=f32)
        grad = grad + jnp.dot(probs_low[BLK:], do, preferred_element_type=f32)
        grad_r = grad_r + jnp.dot(dscores[BLK:], qr, preferred_element_type=f32)
    acc[...] += grad
    acc_r[...] += grad_r

    @pl.when(t == pl.num_programs(1) - 1)
    def _():
        for s in range(4):
            base = s * BLK
            packed = jnp.concatenate(
                [acc_r[base : base + 32, :], acc_r[base + 32 : base + 64, :]], axis=1
            )
            for n in range(18):
                m = n % 9
                if n < 16:
                    l, r = n // 4, n % 4
                    v = acc[base + r * UNIT : base + (r + 1) * UNIT, l * 128 : (l + 1) * 128]
                else:
                    v = packed[(n - 16) * UNIT : (n - 15) * UNIT]
                row = s * HALF + m * UNIT
                units[n // 9, row : row + UNIT, :] = v.astype(bf16)
        part = pl.ds(pl.multiple_of(i * 576, 576), 576)
        gm_ref[part, :] = units[c]
        go_ref[part, :] = units[1 - c]


def attention(meta, lat, rot, mine, other, q, qr, do):
    tiles = BLK * HEADS // TILE
    whole = lambda shape: pl.BlockSpec(shape, lambda i, t: (0, 0))
    rows = lambda width: pl.BlockSpec((TILE, width), lambda i, t: (i * tiles + t, 0))
    return pl.pallas_call(
        attention_kernel,
        grid=(2, tiles),
        out_shape=[
            pltpu.HBM((2 * SEL * BLK, BLK * HEADS), bf16),
            pltpu.HBM((2 * BLK, BLK * HEADS), bf16),
            jax.ShapeDtypeStruct((2 * SEL * BLK, LAT), bf16),
            jax.ShapeDtypeStruct((8 * HALF, 128), bf16),
            jax.ShapeDtypeStruct((8 * HALF, 128), bf16),
        ],
        in_specs=[
            SMEM,
            whole((128, LAT)),
            whole((128, ROPE)),
            whole((8 * HALF, 128)),
            whole((8 * HALF, 128)),
            rows(LAT),
            rows(ROPE),
            rows(LAT),
        ],
        out_specs=[
            pl.BlockSpec((SEL * BLK, TILE), lambda i, t: (i, t)),
            pl.BlockSpec((BLK, TILE), lambda i, t: (i, t)),
            pl.BlockSpec((SEL * BLK, LAT), lambda i, t: (i, 0)),
            whole((8 * HALF, 128)),
            whole((8 * HALF, 128)),
        ],
        scratch_shapes=[
            pltpu.VMEM((2, 576, 128), bf16),
            pltpu.VMEM((SEL * BLK, LAT), bf16),
            pltpu.VMEM((SEL * BLK, ROPE), bf16),
            pltpu.VMEM(((SEL - 1) * BLK, LAT), f32),
            pltpu.VMEM(((SEL - 1) * BLK, ROPE), f32),
        ],
        compiler_params=PARAMS,
        name="attention",
    )(meta, lat, rot, mine, other, q, qr, do)


def output_kernel(probs_ref, ds_ref, keys, q_ref, qr_ref, do_ref, out_ref, dkl_ref, dkr_ref):
    @pl.when(pl.program_id(1) == 0)
    def _():
        dkl_ref[...] = jnp.zeros_like(dkl_ref)
        dkr_ref[...] = jnp.zeros_like(dkr_ref)

    probs = probs_ref[...]
    out_ref[...] = lax.dot_general(
        probs, keys[...], (((0,), (0,)), ((), ())), preferred_element_type=f32
    ).astype(bf16)
    dscores = ds_ref[...]
    dkl_ref[...] += jnp.dot(dscores, q_ref[...], preferred_element_type=f32) + jnp.dot(
        probs[:BLK], do_ref[...], preferred_element_type=f32
    )
    dkr_ref[...] += jnp.dot(dscores, qr_ref[...], preferred_element_type=f32)


def output(probs, ds, keys, q, qr, do):
    tiles = BLK * HEADS // TILE
    rows = lambda width: pl.BlockSpec((TILE, width), lambda i, t: (i * tiles + t, 0))
    return pl.pallas_call(
        output_kernel,
        grid=(2, tiles),
        out_shape=[
            jax.ShapeDtypeStruct(q.shape, bf16),
            jax.ShapeDtypeStruct((2 * BLK, LAT), f32),
            jax.ShapeDtypeStruct((2 * BLK, ROPE), f32),
        ],
        in_specs=[
            pl.BlockSpec((SEL * BLK, TILE), lambda i, t: (i, t)),
            pl.BlockSpec((BLK, TILE), lambda i, t: (i, t)),
            pl.BlockSpec((SEL * BLK, LAT), lambda i, t: (i, 0)),
            rows(LAT),
            rows(ROPE),
            rows(LAT),
        ],
        out_specs=[
            rows(LAT),
            pl.BlockSpec((BLK, LAT), lambda i, t: (i, 0)),
            pl.BlockSpec((BLK, ROPE), lambda i, t: (i, 0)),
        ],
        compiler_params=PARAMS,
        name="output",
    )(probs, ds, keys, q, qr, do)


def slots_kernel(mine, recv, g):
    g[0:1152] = mine[...]
    g[1152:2304] = recv[...]


def plane_kernel(where_, *refs):
    ins, rest, own, acc = refs[:4], refs[4:8], refs[8:12], refs[12]
    acc[...] = jnp.zeros_like(acc)
    for k in range(4):
        for s in range(16):
            f = where_[k * 16 + s]
            acc[f] = acc[f] + ins[k][s * HALF : (s + 1) * HALF].astype(f32)
    for k in range(4):
        for j in range(16):
            out, row = (own[k], j) if j < 4 else (rest[k], j - 4)
            out[row * HALF : (row + 1) * HALF] = acc[ORDER[k] * 16 + j].astype(out.dtype)


def sum_rows(ins, at):
    total = ins[0][at : at + HALF].astype(f32)
    for part in ins[1:]:
        total = total + part[at : at + HALF].astype(f32)
    return total


def column_kernel(*refs):
    ins, outs = refs[:4], refs[4:7]
    for j in range(12):
        out, row = outs[ORDER.index(j // 4 + 1) - 1], (j % 4) * HALF
        out[row : row + HALF] = sum_rows(ins, j * HALF).astype(bf16)


def owner_kernel(*refs):
    ins, outs = refs[:7], refs[7:9]
    for j in range(4):
        row = (j % 2) * HALF
        outs[j // 2][row : row + HALF] = sum_rows(ins, j * HALF)


def half_sum_kernel(meta, mine, recv, dkl, dkr, out, units):
    c = meta[0]
    units[c] = mine[...]
    units[1 - c] = recv[...]
    for i in range(2):
        lo, hi = slice(i * 64, i * 64 + 32), slice(i * 64 + 32, i * 64 + 64)
        packed = jnp.concatenate([dkr[lo, :], dkr[hi, :]], axis=1)
        for n in range(18):
            if n < 16:
                l, r = n // 4, n % 4
                own = dkl[i * 64 + r * UNIT : i * 64 + (r + 1) * UNIT, l * 128 : (l + 1) * 128]
            else:
                own = packed[(n - 16) * UNIT : (n - 15) * UNIT]
            row = i * HALF + (n % 9) * UNIT
            to = (i * 18 + n) * UNIT
            out[to : to + UNIT] = (units[n // 9, row : row + UNIT, :] + own).astype(bf16)


def final_kernel(mine, recv, cosine, sine, lat_out, rope_out):
    parts = []
    for i in range(2):
        for n in range(16):
            l, r = n // 4, n % 4
            at = (i * 18 + n) * UNIT
            lat_out[i * 64 + r * UNIT : i * 64 + (r + 1) * UNIT, l * 128 : (l + 1) * 128] = mine[
                at : at + UNIT
            ].astype(f32) + recv[at : at + UNIT].astype(f32)
        at = (i * 18 + 16) * UNIT
        packed = mine[at : at + 32].astype(f32) + recv[at : at + 32].astype(f32)
        parts += [packed[:, :64], packed[:, 64:]]
    g = jnp.concatenate(parts, axis=0).T
    lo, hi, cs, sn = g[:32], g[32:], cosine[...], sine[...]
    rope_out[...] = jnp.concatenate([lo * cs + hi * sn, hi * cs - lo * sn], axis=0)


def shards(latent, rope_key, queries, query_rope, grad_out, sel_blocks):
    x, y, z, c = [lax.axis_index(a) for a in "xyzc"]
    ctx = ((x * 4 + y) * 4 + z) * 2 + c
    meta = jnp.stack([c, ctx * 2]).astype(jnp.int32)

    positions = ctx * 128 + jnp.arange(128, dtype=jnp.int32)
    freq_steps = jnp.arange(ROPE // 2, dtype=f32)
    inverse_freq = rope_base ** (-2.0 * freq_steps / ROPE)
    angles = positions.astype(f32)[None, :] * inverse_freq[:, None]
    cosine, sine = jnp.cos(angles), jnp.sin(angles)

    sel_row = sel_blocks[:, 1:].reshape(1, 8).astype(bf16)
    sel_unit = jnp.broadcast_to(jnp.pad(sel_row, ((0, 0), (0, 120))), (UNIT, 128))
    mine, other, rot = call(
        prep_kernel,
        (meta, latent, rope_key.T, cosine, sine, sel_unit),
        [((304, 128), bf16), ((304, 128), bf16), ((128, ROPE), bf16)],
        [pltpu.VMEM((2, 304, 128), bf16)],
        scalars=1,
        name="prep",
    )
    chip, sel = call(
        chip_kernel, (mine, swap(other, "c")), [((576, 128), bf16), ((UNIT, 128), bf16)], name="chip"
    )

    def all_of(a, phase):
        return [a] + [exchange(a, phase, k) for k in (1, 2, 3)]

    def each_of(parts, phase):
        return [exchange(part, phase, k) for part, k in zip(parts, ORDER[1:])]

    own_plane = all_of(chip, "v")
    lines = all_of(chip, "u")
    got = lax.optimization_barrier((*own_plane[1:], *lines[1:]))
    own_plane = [chip, *got[:3]]
    (line,) = call(line_kernel, got[3:], [((1728, 128), bf16)], name="line")
    rest_plane = all_of(line, "v")

    asked = jnp.stack([t[:2, :8] for t in all_of(sel, "w")]).astype(jnp.int32).reshape(4, 16)
    sx, sy, sz = asked >> 6, (asked >> 4) & 3, (asked >> 2) & 3
    local = jnp.where(((asked >> 1) & 1) == c, 0, 2) + (asked & 1)
    on_v = jnp.where(c == 0, x ^ sx, y ^ sy)
    on_w = jnp.where(c == 0, y ^ sy, x ^ sx)
    pos = on_v * 16 + (z ^ sz) * 4 + local
    pack_at = pos.reshape(-1)
    add_at = jnp.where(on_w == 0, pos, 64).reshape(-1)
    merge_at = on_w[0]

    packed = call(
        pack_kernel,
        [pack_at] + own_plane + rest_plane,
        [((2304, 128), bf16)] * 4,
        [pltpu.VMEM((64, HALF, 128), bf16)],
        scalars=1,
        name="pack",
    )
    got = [packed[0]] + each_of(packed[1:], "w")
    key_mine, key_other = call(
        merge_kernel,
        [merge_at] + got,
        [((8 * HALF, 128), bf16)] * 2,
        [pltpu.VMEM((64, HALF, 128), bf16)],
        scalars=1,
        name="merge",
    )
    key_recv = swap(key_other, "c")

    q = queries.reshape(128 * HEADS, LAT)
    do = grad_out.reshape(128 * HEADS, LAT)
    qr = query_rope.reshape(128 * HEADS, ROPE)
    probs, ds, keys, g_mine, g_other = attention(meta, latent, rot, key_mine, key_recv, q, qr, do)

    (slots,) = call(slots_kernel, (g_mine, swap(g_other, "c")), [((2304, 128), bf16)], name="slots")
    keys, slots = lax.optimization_barrier((keys, slots))
    out, dkl, dkr = output(probs, ds, keys, q, qr, do)
    add_at, dkl, dkr = lax.optimization_barrier((add_at, dkl, dkr))
    sums = call(
        plane_kernel,
        [add_at] + all_of(slots, "w"),
        [((rows, 128), bf16 if k else f32) for rows in (1728, 576) for k in range(4)],
        [pltpu.VMEM((65, HALF, 128), f32)],
        scalars=1,
        name="plane",
    )
    rest, own = sums[:4], sums[4:]
    columns = call(
        column_kernel, [rest[0]] + each_of(rest[1:], "v"), [((576, 128), bf16)] * 3, name="column"
    )
    got = [own[0]] + each_of(own[1:], "v") + each_of(columns, "u")
    f_mine, f_other = call(owner_kernel, got, [((288, 128), f32)] * 2, name="owner")
    (total,) = call(
        half_sum_kernel,
        (meta, f_mine, swap(f_other, "c"), dkl, dkr),
        [((576, 128), bf16)],
        [pltpu.VMEM((2, 288, 128), f32)],
        scalars=1,
        name="half_sum",
    )
    d_latent, d_rope_key = call(
        final_kernel,
        (total, swap(total, "h"), cosine, sine),
        [((128, LAT), f32), ((ROPE, 128), f32)],
        name="final",
    )
    return out.reshape(128, HEADS, LAT), d_latent, d_rope_key.T


def solution(mesh):
    lines = Mesh(mesh.devices.reshape(4, 4, 4, 2, 2), MESH)
    ctx = ("x", "y", "z", "c")
    return jax.shard_map(
        shards,
        mesh=lines,
        in_specs=(
            P(ctx, None),
            P(ctx, None),
            P(ctx, "h", None),
            P(ctx, "h"),
            P(ctx, "h", None),
            P(ctx, None),
        ),
        out_specs=(P(ctx, "h", None), P(ctx, None), P(ctx, None)),
        check_vma=False,
    )
```
